768 devices in a mesh: lat: 48 (over z, x_lo, core), fld: 16 (over x_hi, y).
Axes of the slice: x: 4 (x_hi: 2, x_lo: 2; x = x_hi * 2 + x_lo), y: 8, z: 12, core: 2. Of those that a mesh axis runs over, the one named last changes fastest.
Arguments:
- spectral: bfloat16 [768, 2, 16, 72, 640], P('lat', None, 'fld'), may hold values from -6 to 6
- legendre: bfloat16 [768, 96, 640], P('lat'), may hold values from -0.0078125 to 0.0078125
- wave_slot: int32 [768], replicated, may hold values from 0 to 767, each once
- coupling_in: bfloat16 [1044, 16], replicated, may hold values from -1.5 to 1.5
- interaction: bfloat16 [1044, 1044], replicated, may hold values from -0.1875 to 0.1875
- bin_speed: float32 [1044], replicated, may hold values from 0.02 to 0.2
- momentum: float32 [1044], replicated, may hold values from -1 to 1
- wave_state: bfloat16 [1044, 98304], P(None, ('lat', 'fld')), may hold values from 0.099609375 to 1
- cell_index: int32 [98304], P('lat'), may hold values from 0 to 245759
- edge_source: int32 [393216], P(('lat', 'fld')), may hold values from 0 to 255
- edge_target: int32 [393216], P(('lat', 'fld')), may hold values from 0 to 127
- surface_drag: float32 [16], P('fld'), may hold values from -4 to 4
- mixing: float32 [72], replicated, may hold values from 0.05 to 2
Outputs:
- mixed: bfloat16 [96, 16, 72, 2560], P('lat', 'fld')
- wave_next: bfloat16 [1044, 98304], P(None, ('lat', 'fld'))
The draws below stay inside these ranges and needn't reach their ends.
Inputs may be any that keep to these rules, and one draw needn't show every extreme that they name: `wave_slot`: each slot holds a different wavenumber. `edge_source`: values below 64 name the previous tile's last points, values from 192 on the next tile's first points.
All inputs are finite; a program needn't handle non-finite values.
Results may differ from the reference program's by a relative error of at most 0.0085.
Values may be sent and summed in bfloat16 or wider, within the bound.
No kernel may reach another device: no remote copies, remote signals or barrier semaphores. Data moves between devices by JAX's collectives and lax.ppermute only.
A program may use at most 64 MiB of HBM per device.

```python
import math
import jax
import jax.numpy as jnp
from jax import lax

M = 768
NDEG = 640
LON = 2560
FIELDS = 16
LEV = 72
NB = 1044
RIM = 64
WP_DEV = 128
EDGES_DEV = 512
LAT = 96
WP = 98304
EDGES = 393216
N_LAT = 48
N_FLD = 16


def with_ends(result, key, smallest, top_value):
    dims = result.shape
    spot = [jax.random.randint(jax.random.fold_in(key, axis), (), 0, dims[axis]) for axis in range(len(dims))]
    result = result.at[tuple(spot)].set(smallest)
    longest = dims.index(max(dims))
    spot[longest] = (spot[longest] + 1) % dims[longest]
    return result.at[tuple(spot)].set(top_value)


def shard_levels(stream_key, extent, shards, smallest, top_value):
    def one(position, blocks):
        steps = jax.random.uniform(jax.random.fold_in(jax.random.fold_in(stream_key, 6), position), (blocks,), jnp.float32, smallest / len(shards), top_value / len(shards))
        return jnp.repeat(jnp.exp(steps), extent[position] // blocks).reshape((-1,) + (1,) * (len(extent) - position - 1))

    factor_of = one(*shards[0])
    for cut in shards[1:]:
        factor_of = factor_of * one(*cut)
    return factor_of


def centred(own_key, shape, width, limit, cuts=(), kind=jnp.bfloat16):
    loudness = shard_levels(own_key, shape, cuts, -0.22, 0.18) if cuts else 1.0
    array = jax.random.normal(own_key, shape, jnp.float32) * width * loudness
    return jnp.minimum(jnp.maximum(array, -limit), limit).astype(kind)


def setup_inputs(seed: int = 0) -> dict:
    seeds = jax.random.split(jax.random.key(seed), 14)
    spectral = centred(seeds[0], (M, 2, FIELDS, LEV, NDEG), 1.0, 6.0, ((0, 48), (2, 16)))
    legendre = centred(seeds[1], (M, LAT, NDEG), (NDEG * M) ** -0.5, 0.0078125, ((0, 48),))
    wave_slot = jax.random.permutation(seeds[2], M).astype(jnp.int32)
    coupling_in = centred(seeds[3], (NB, FIELDS), FIELDS ** -0.5, 1.5)
    interaction = centred(seeds[4], (NB, NB), NB ** -0.5, 0.1875)
    bin_speed = jnp.clip(jnp.exp(jax.random.uniform(seeds[5], (NB,), jnp.float32, math.log(0.02), math.log(0.2))), 0.02, 0.2)
    momentum = centred(seeds[6], (NB,), (NB // 32) ** -0.5, 1.0, (), jnp.float32)
    wave_state = jnp.clip(0.099609375 + 0.9003906 * jax.random.uniform(seeds[7], (NB, WP), jnp.float32) ** shard_levels(seeds[7], (NB, WP), ((1, 768),), -0.2, 0.2), 0.099609375, 1.0).astype(jnp.bfloat16)
    cell_index = with_ends(jax.random.randint(seeds[8], (WP,), 0, LAT * LON), jax.random.fold_in(seeds[8], 1), 0, (LAT * LON) - 1).astype(jnp.int32)
    edge_source = with_ends(jax.random.randint(seeds[9], (EDGES,), 0, WP_DEV + 2 * RIM), jax.random.fold_in(seeds[9], 1), 0, (WP_DEV + 2 * RIM) - 1).astype(jnp.int32)
    edge_target = with_ends(jax.random.randint(seeds[10], (EDGES,), 0, WP_DEV), jax.random.fold_in(seeds[10], 1), 0, WP_DEV - 1).astype(jnp.int32)
    surface_drag = centred(seeds[11], (FIELDS,), 1.0, 4.0, ((0, 16),), jnp.float32)
    mixing = jnp.clip(jnp.exp(jax.random.uniform(seeds[12], (LEV,), jnp.float32, math.log(0.05), math.log(2.0))), 0.05, 2.0)
    return dict(spectral=spectral, legendre=legendre, wave_slot=wave_slot, coupling_in=coupling_in, interaction=interaction, bin_speed=bin_speed, momentum=momentum, wave_state=wave_state, cell_index=cell_index, edge_source=edge_source, edge_target=edge_target, surface_drag=surface_drag, mixing=mixing)


time_step = 0.25

def wave_angles(wave_slot, longitudes):
    column = jnp.arange(longitudes, dtype=jnp.int32)
    phases = (wave_slot[:, None] * column[None, :] % longitudes).astype(jnp.float32)
    angles = phases * (2.0 * jnp.pi / longitudes)
    return jnp.stack([jnp.cos(angles), -jnp.sin(angles)], axis=1).astype(jnp.bfloat16)

def reference(spectral, legendre, wave_slot, coupling_in, interaction, bin_speed, momentum, wave_state, cell_index, edge_source, edge_target, surface_drag, mixing):
    limits = NDEG - wave_slot * NDEG // M
    live_mask = (jnp.arange(NDEG, dtype=jnp.int32)[None, :] < limits[:, None]).astype(jnp.bfloat16)

    def one_slot(slot_index):
        weights = legendre[slot_index].astype(jnp.float32)
        coeffs = (spectral[slot_index] * live_mask[slot_index][None, None, None, :]).astype(jnp.float32)
        return jnp.einsum('tn,cfln->tcfl', weights, coeffs, precision=lax.Precision.HIGHEST).astype(jnp.bfloat16)
    fourier = lax.map(one_slot, jnp.arange(M, dtype=jnp.int32))
    wave_table = wave_angles(wave_slot, LON).astype(jnp.float32)

    def one_row(row_index):
        pieces = fourier[:, row_index].astype(jnp.float32)
        return jnp.einsum('scfl,scj->flj', pieces, wave_table, precision=lax.Precision.HIGHEST).astype(jnp.bfloat16)
    grid_rows = lax.map(one_row, jnp.arange(LAT, dtype=jnp.int32))
    surface = grid_rows[:, :, LEV - 1, :].transpose(1, 0, 2).reshape(FIELDS, LAT * LON)
    forcing = surface[:, cell_index]
    growth = jnp.tanh(jnp.dot(coupling_in.astype(jnp.float32), forcing.astype(jnp.float32), preferred_element_type=jnp.float32))
    current = wave_state.astype(jnp.float32)
    padded = jnp.pad(current, ((0, 0), (RIM, RIM)))

    def tile_flux(tile_index):
        extended = lax.dynamic_slice_in_dim(padded, tile_index * WP_DEV, WP_DEV + 2 * RIM, 1)
        own_points = lax.dynamic_slice_in_dim(current, tile_index * WP_DEV, WP_DEV, 1)
        sources = lax.dynamic_slice_in_dim(edge_source, tile_index * EDGES_DEV, EDGES_DEV)
        targets = lax.dynamic_slice_in_dim(edge_target, tile_index * EDGES_DEV, EDGES_DEV)
        change = extended[:, sources] - own_points[:, targets]
        return jnp.zeros((NB, WP_DEV), jnp.float32).at[:, targets].add(change)
    flux = lax.map(tile_flux, jnp.arange(N_LAT * N_FLD, dtype=jnp.int32))
    flux = flux.transpose(1, 0, 2).reshape(NB, WP)
    advected = current + bin_speed[:, None] * flux
    squared = (advected * advected).astype(jnp.bfloat16)
    transfer = jnp.dot(interaction.astype(jnp.float32), squared.astype(jnp.float32), preferred_element_type=jnp.float32)
    wave_new = advected + time_step * (growth * advected + transfer)
    stress = jnp.sum(momentum[:, None] * growth * wave_new, axis=0)
    stress_grid = jnp.zeros((LAT * LON,), jnp.float32).at[cell_index].add(stress).reshape(LAT, LON)
    zero_one = jnp.zeros((1,), jnp.float32)
    upper_band = jnp.concatenate([-mixing[:-1], zero_one])
    lower_band = jnp.concatenate([zero_one, -mixing[:-1]])
    middle = 1.0 + mixing + jnp.concatenate([zero_one, mixing[:-1]])
    solve_shape = (FIELDS, LEV)

    def one_mix(row_index):
        right_side = grid_rows[row_index].astype(jnp.float32)
        right_side = right_side.at[:, LEV - 1, :].add(surface_drag[:, None] * stress_grid[row_index][None, :])
        solved = lax.linalg.tridiagonal_solve(jnp.broadcast_to(lower_band, solve_shape), jnp.broadcast_to(middle, solve_shape), jnp.broadcast_to(upper_band, solve_shape), right_side)
        return solved.astype(jnp.bfloat16)
    mixed = lax.map(one_mix, jnp.arange(LAT, dtype=jnp.int32))
    return (mixed, wave_new.astype(jnp.bfloat16))
```

```python
import functools

import jax
import jax.numpy as jnp
from jax import lax
from jax.experimental import pallas as pl
from jax.experimental.pallas import tpu as pltpu
from jax.sharding import PartitionSpec as P

LON = 2560
RIM = 64
QUARTER = LON // 4
LANES = 128

time_step = 0.25

bf16 = jnp.bfloat16
f32 = jnp.float32
i32 = jnp.int32

NN = (((1,), (0,)), ((), ()))
NT = (((1,), (1,)), ((), ()))

VMEM = pl.BlockSpec(memory_space=pltpu.VMEM)
SMEM = pl.BlockSpec(memory_space=pltpu.SMEM)


def dot(a, b, dims=NN):
    return lax.dot_general(a, b, dims, preferred_element_type=f32)


def lane_of(shape):
    return lax.broadcasted_iota(i32, shape, len(shape) - 1)


def params(mib, **more):
    return pltpu.CompilerParams(vmem_limit_bytes=mib << 20, **more)


def cost(flops, nbytes, trans=0):
    return pl.CostEstimate(flops=int(flops), bytes_accessed=int(nbytes), transcendentals=int(trans))


def legendre_kernel(per, slots, lats, levels, limit_ref, leg_ref, spec_ref, f0_ref, f1_ref, x_ref, s0, s1, low):
    step = pl.program_id(0)

    @pl.when(step == 0)
    def _():
        low[...] = jnp.zeros_like(low)

    degrees = leg_ref.shape[2]
    column = lane_of((1, degrees))
    lane = lane_of((lats, LANES))
    picked = low[0:lats, :]
    fill = jnp.zeros((lats, LANES - levels), f32)
    for k in range(per):
        slot = step * per + k
        live = column < limit_ref[slot]
        weights = jnp.where(live, leg_ref[k].astype(f32), 0.0).astype(bf16)
        for c, store in ((0, s0), (1, s1)):
            sums = dot(weights, spec_ref[k, c, 0], NT)
            store[pl.ds(slot, lats, stride=slots), :] = jnp.concatenate([sums, fill], axis=1)
            lowest = jnp.broadcast_to(sums[:, levels - 1 : levels], (lats, LANES))
            picked = jnp.where(lane == c * slots + slot, lowest, picked)
    low[0:lats, :] = picked

    @pl.when(step == pl.num_programs(0) - 1)
    def _():
        f0_ref[...] = s0[:, 0:levels].astype(bf16)
        f1_ref[...] = s1[:, 0:levels].astype(bf16)
        turned = low[...].T
        tail = turned[24:32, :]
        lane8 = lane_of((8, LANES))
        rows = [
            jnp.where(lane8 < 96, turned[8 * h : 8 * h + 8, :], pltpu.roll(tail, 96 - 32 * h, 1))
            for h in range(3)
        ]
        packed = jnp.concatenate(rows, axis=0).astype(bf16)
        x_ref[...] = jnp.broadcast_to(packed[None], x_ref.shape)


def inverse_kernel(levels, mix_ref, w_ref, col_ref, left, right):
    width = 2 * LANES
    lane = lax.broadcasted_iota(i32, (2, width), 1)
    start = lax.broadcasted_iota(i32, (2, width), 0) * levels
    unit = lane - start
    ratio, part = [], []
    for level in range(levels):
        below = jnp.full((2, width), mix_ref[level], f32)
        rhs = (unit == level).astype(f32)
        if level == 0:
            scale = 1.0 / (1.0 + below)
            part.append(rhs * scale)
        else:
            above = jnp.full((2, width), mix_ref[level - 1], f32)
            scale = 1.0 / (1.0 + below + above - above * ratio[-1])
            part.append((rhs + above * part[-1]) * scale)
        ratio.append(below * scale)
    solved = part[-1]
    for level in range(levels - 1, -1, -1):
        if level < levels - 1:
            solved = part[level] + ratio[level] * solved
        left[2 * level : 2 * level + 2, :] = solved[:, :LANES]
        right[2 * level : 2 * level + 2, :] = solved[:, LANES:]
    for c in range(2):
        block = jnp.concatenate([half[pl.ds(c, levels, stride=2), :] for half in (left, right)], axis=1)
        high = block.astype(bf16)
        w_ref[2 * c] = high
        w_ref[2 * c + 1] = (block - high.astype(f32)).astype(bf16)
        if c == 0:
            col_ref[...] = jnp.broadcast_to(block[:, levels - 1 : levels], col_ref.shape)


def mix_kernel(owners, f0_ref, f1_ref, w_ref, codes_ref, o_ref, rest):
    sums = dot(f0_ref[...], w_ref[0]) + dot(f0_ref[...], w_ref[1])
    sums += dot(f1_ref[...], w_ref[2]) + dot(f1_ref[...], w_ref[3])
    count = sums.shape[0]
    rest[...] = sums[:, LANES:]
    lane = lane_of((count // 4, LANES))
    tail = jnp.broadcast_to(codes_ref[...][None], (owners, 8, LANES)).reshape(count // 4, LANES)
    for g in range(4):
        piece = rest[pl.ds(g, count // 4, stride=4), :]
        if g:
            piece = pltpu.roll(piece, 16 * g, 1)
        tail = jnp.where((lane >= 16 * g) & (lane < 16 * g + 16), piece, tail)
    whole = jnp.concatenate(
        [sums[:, :LANES].reshape(owners, count // owners, LANES), tail.reshape(owners, 8, LANES)], axis=1
    )
    o_ref[...] = whole.astype(bf16)


def table_kernel(slots, bc_ref, bs_ref, ac_ref, as_ref, cc_ref, cs_ref, long_ref, wide_ref):
    bc, bs = bc_ref[...], bs_ref[...]
    for a in range(QUARTER // LANES):
        ca, sa = ac_ref[a : a + 1, :], as_ref[a : a + 1, :]
        rows = slice(a * LANES, (a + 1) * LANES)
        long_ref[rows, 0:slots] = (ca * bc - sa * bs).astype(bf16)
        long_ref[rows, slots : 2 * slots] = (-(sa * bc + ca * bs)).astype(bf16)
    for first in range(0, slots, LANES):
        mine = slice(first, first + LANES)
        tc, ts = bc[:, mine].T, bs[:, mine].T
        for a in range(QUARTER // LANES):
            ca, sa = cc_ref[mine, a : a + 1], cs_ref[mine, a : a + 1]
            columns = slice(a * LANES, (a + 1) * LANES)
            wide_ref[mine, columns] = (ca * tc - sa * ts).astype(bf16)
            wide_ref[slots + first : slots + first + LANES, columns] = (-(sa * tc + ca * ts)).astype(bf16)


def turned_pair(first, second, wave, m):
    if m == 0:
        return first, second
    turns = (wave * m) & 3
    even = (turns & 1) == 0
    sign0 = jnp.where((turns == 0) | (turns == 3), 1.0, -1.0)
    sign1 = jnp.where((turns == 0) | (turns == 1), 1.0, -1.0)
    return jnp.where(even, first, second) * sign0, jnp.where(even, second, first) * sign1


def surface_kernel(slots, x_ref, long_ref, wave_ref, row_ref, hot_ref, o_ref, surface, picked):
    peers = x_ref.shape[0]
    x = x_ref[...].astype(f32)
    lane = lane_of((peers, 8, LANES))
    tail = jnp.zeros((peers, 8, LANES), f32)
    for h in range(3):
        moved = pltpu.roll(x[:, 8 * h : 8 * h + 8, :].reshape(peers * 8, LANES), 32 + 32 * h, 1)
        tail = jnp.where((lane >= 32 * h) & (lane < 32 * h + 32), moved.reshape(peers, 8, LANES), tail)
    real = x[:, 0:16, :].reshape(slots, LANES)
    imaginary = jnp.concatenate([x[:, 16:24, :], tail], axis=1).reshape(slots, LANES)
    wave = jnp.broadcast_to(wave_ref[...], (slots, LANES))
    pairs = [turned_pair(real, imaginary, wave, m) for m in range(4)]
    coefficients = jnp.concatenate(
        [jnp.concatenate([p[c].astype(bf16) for p in pairs], axis=1) for c in range(2)], axis=0
    )
    values = dot(long_ref[...], coefficients).astype(bf16).astype(f32)
    for m in range(4):
        surface[m * QUARTER : (m + 1) * QUARTER, :] = values[:, m * LANES : (m + 1) * LANES]

    def fetch(block, carry):
        for u in range(32):
            p = block * 32 + u
            picked[pl.ds(p, 1), :] = surface[pl.ds(row_ref[p], 1), :]
        return carry

    points = hot_ref.shape[0]
    lax.fori_loop(0, points // 32, fetch, 0)
    chosen = (picked[...] * hot_ref[...].astype(f32)).astype(bf16)
    lined = dot(jnp.ones((8, LANES), bf16), chosen, NT)
    rows = [lined[0:1, k * LANES : (k + 1) * LANES] for k in range(points // LANES)]
    o_ref[...] = jnp.concatenate(rows, axis=0).astype(bf16)


def advect_kernel(state_ref, rims_ref, source_ref, target_ref, speed_ref, inter_ref, adv_ref, base_ref):
    edges = source_ref.shape[1]
    points = state_ref.shape[1]
    source_hot = (lax.broadcasted_iota(i32, (points + 2 * RIM, edges), 0) == source_ref[...]).astype(f32)
    target_hot = (lax.broadcasted_iota(i32, (points, edges), 0) == target_ref[...]).astype(f32)
    source_hot, target_hot = source_hot.astype(bf16), target_hot.astype(bf16)
    routes = dot(source_hot, target_hot, NT)
    counts = dot(jnp.ones((8, edges), bf16), target_hot, NT)[0:1, :]
    rim_routes = jnp.concatenate([routes[0:RIM], routes[RIM + points :]], axis=0)
    own_routes = routes[RIM : RIM + points]
    inflow = None
    for values, table in ((state_ref[...], own_routes), (rims_ref[...], rim_routes)):
        high = table.astype(bf16)
        rest = (table - high.astype(f32)).astype(bf16)
        part = dot(values, high) + dot(values, rest)
        inflow = part if inflow is None else inflow + part
    current = state_ref[...].astype(f32)
    advected = current + speed_ref[...] * (inflow - counts * current)
    squared = (advected * advected).astype(bf16)
    transfer = dot(inter_ref[...], squared)
    adv_ref[...] = time_step * advected
    base_ref[...] = advected + time_step * transfer


def wave_kernel(forcing_ref, coupling_ref, adv_ref, base_ref, momentum_ref, next_ref, stress_ref):
    growth = jnp.tanh(dot(coupling_ref[...], forcing_ref[...]))
    wave_new = base_ref[...] + growth * adv_ref[...]
    next_ref[...] = wave_new.astype(bf16)
    stress = jnp.sum(momentum_ref[...] * growth * wave_new, axis=0, keepdims=True)
    stress_ref[...] = jnp.broadcast_to(stress, stress_ref.shape)


def synthesis_kernel(
    slots, levels, y_ref, wave_ref, wide_ref, base_ref, d_ref, high_ref, hot_ref, rest, tails, lhs
):
    peers = y_ref.shape[0]
    y = y_ref[...].astype(f32)
    main = y[:, 0:32, :]
    tail = y[:, 32:40, :].reshape(peers * 8, LANES)
    tails[...] = tail
    for g in range(4):
        rest[pl.ds(g, peers * 8, stride=4), :] = pltpu.roll(tail, LANES - 16 * g, 1) if g else tail
    wave = wave_ref[...]
    others = rest[...].reshape(peers, 32, LANES)
    padded = 80
    fill = jnp.zeros((padded - levels, slots), f32)
    for t in range(2):
        a = main[:, 16 * t : 16 * t + 16, :].reshape(slots, LANES).T
        b = others[:, 16 * t : 16 * t + 16, :].reshape(slots, LANES).T
        first = a[0:levels]
        second = jnp.concatenate([a[levels:], b[0 : 2 * levels - LANES]], axis=0)
        for m in range(4):
            p, q = turned_pair(first, second, wave, m)
            rows = slice((t * 4 + m) * padded, (t * 4 + m + 1) * padded)
            lhs[rows, 0:slots] = jnp.concatenate([p, fill], axis=0).astype(bf16)
            lhs[rows, slots : 2 * slots] = jnp.concatenate([q, fill], axis=0).astype(bf16)
    for t in range(2):
        sums = dot(lhs[t * 4 * padded : (t + 1) * 4 * padded, :], wide_ref[...])
        for m in range(4):
            d_ref[t, :, m * QUARTER : (m + 1) * QUARTER] = sums[m * padded : m * padded + levels]
    lane = lane_of((peers, LANES))
    parts = []
    for v in range(3):
        left = pltpu.roll(tails[pl.ds(2 * v, peers, stride=8), :], 64, 1)
        parts.append(jnp.where(lane < 64, left, tails[pl.ds(2 * v + 1, peers, stride=8), :]))
    cell = (parts[0] * 65536.0 + parts[1] * 256.0 + parts[2]).astype(i32) - base_ref[0]
    high_ref[...] = cell >> 7
    at = cell & (LANES - 1)
    row = lax.broadcasted_iota(i32, (LANES, LANES), 0)
    for k in range(peers):
        hot_ref[:, k * LANES : (k + 1) * LANES] = (row == at[k : k + 1, :]).astype(f32).astype(bf16)


def scatter_kernel(stress_ref, high_ref, hot_ref, o_ref):
    peers = stress_ref.shape[0]
    height = o_ref.shape[1]
    row = lax.broadcasted_iota(i32, (height, LANES), 0)
    first, second = [], []
    for k in range(peers):
        spread = jnp.where(row == high_ref[k : k + 1, :], stress_ref[k : k + 1, :], 0.0)
        high = spread.astype(bf16)
        first.append(high)
        second.append((spread - high.astype(f32)).astype(bf16))
    hot = hot_ref[...]
    sums = dot(jnp.concatenate(first, axis=1), hot, NT) + dot(jnp.concatenate(second, axis=1), hot, NT)
    o_ref[...] = jnp.broadcast_to(sums.astype(bf16)[None], o_ref.shape)


def final_kernel(d_ref, part_ref, col_ref, drag_ref, o_ref):
    stress = jnp.sum(part_ref[...].astype(f32), axis=0)
    push = col_ref[...] * drag_ref[0]
    chunks = LON // LANES
    for t in range(2):
        for k in range(chunks):
            columns = slice(k * LANES, (k + 1) * LANES)
            line = stress[t * chunks + k : t * chunks + k + 1, :]
            o_ref[t, 0, :, columns] = (d_ref[t, :, columns] + push * line).astype(bf16)


def local(
    spectral,
    legendre,
    wave_slot,
    coupling_in,
    interaction,
    bin_speed,
    momentum,
    wave_state,
    cell_index,
    edge_source,
    edge_target,
    surface_drag,
    mixing,
):
    slots, _, _, levels, degrees = spectral.shape
    lats = legendre.shape[1]
    all_slots = wave_slot.shape[0]
    owners = lax.axis_size("lat")
    columns = lax.axis_size("fld")
    bins, points = wave_state.shape
    lat, fld = lax.axis_index("lat"), lax.axis_index("fld")
    shape = jax.ShapeDtypeStruct

    own_slots = lax.dynamic_slice_in_dim(wave_slot, lat * slots, slots)
    limits = degrees - own_slots * degrees // all_slots
    per = 4
    f0, f1, lowest = pl.pallas_call(
        functools.partial(legendre_kernel, per, slots, lats, levels),
        grid=(slots // per,),
        in_specs=[
            SMEM,
            pl.BlockSpec((per, lats, degrees), lambda i: (i, 0, 0)),
            pl.BlockSpec((per, 2, 1, levels, degrees), lambda i: (i, 0, 0, 0, 0)),
        ],
        out_specs=[
            pl.BlockSpec((lats * slots, levels), lambda i: (0, 0)),
            pl.BlockSpec((lats * slots, levels), lambda i: (0, 0)),
            pl.BlockSpec((owners, 24, LANES), lambda i: (0, 0, 0)),
        ],
        out_shape=[
            shape((lats * slots, levels), bf16),
            shape((lats * slots, levels), bf16),
            shape((owners, 24, LANES), bf16),
        ],
        scratch_shapes=[
            pltpu.VMEM((lats * slots, LANES), f32),
            pltpu.VMEM((lats * slots, LANES), f32),
            pltpu.VMEM((LANES, LANES), f32),
        ],
        compiler_params=params(16),
        cost_estimate=cost(3e8, 5e6),
        name="legendre",
    )(limits, legendre, spectral)
    gathered = lax.all_to_all(lowest, "lat", split_axis=0, concat_axis=0, tiled=True)

    tiles = owners * columns
    up = [(k, k + 1) for k in range(tiles - 1)]
    low = lax.ppermute(wave_state[:, points - RIM :], ("lat", "fld"), up)
    high = lax.ppermute(wave_state[:, :RIM], ("lat", "fld"), [(b, a) for a, b in up])

    mixers, column = pl.pallas_call(
        functools.partial(inverse_kernel, levels),
        in_specs=[SMEM],
        out_specs=[VMEM, VMEM],
        out_shape=[shape((4, levels, 2 * LANES), bf16), shape((levels, LANES), f32)],
        scratch_shapes=[pltpu.VMEM((2 * levels, LANES), f32)] * 2,
        compiler_params=params(8),
        cost_estimate=cost(3e6, 2e5),
        name="inverse",
    )(mixing)
    own_cells = lax.dynamic_slice_in_dim(cell_index, fld * points, points)
    codes = jnp.stack([own_cells >> 16, (own_cells >> 8) & 255, own_cells & 255])
    codes = jnp.pad(codes.astype(f32).reshape(6, 64), ((0, 2), (64, 0)))
    packed = pl.pallas_call(
        functools.partial(mix_kernel, owners),
        in_specs=[VMEM] * 4,
        out_specs=VMEM,
        out_shape=shape((owners, 40, LANES), bf16),
        scratch_shapes=[pltpu.VMEM((lats * slots, LANES), f32)],
        compiler_params=params(16),
        cost_estimate=cost(2e8, 2e6),
        name="mix",
    )(f0, f1, mixers, codes)
    bulk = lax.all_to_all(packed, "lat", split_axis=0, concat_axis=0, tiled=True)

    def angles(steps):
        phase = (steps % LON).astype(f32) * (2.0 * jnp.pi / LON)
        return jnp.cos(phase), jnp.sin(phase)

    coarse = jnp.arange(8, dtype=i32) * LANES
    fine = jnp.concatenate([jnp.arange(LANES, dtype=i32), coarse])
    rows_cos, rows_sin = angles(fine[:, None] * wave_slot[None, :])
    cols_cos, cols_sin = angles(wave_slot[:, None] * coarse[None, :])
    long, wide = pl.pallas_call(
        functools.partial(table_kernel, all_slots),
        in_specs=[VMEM] * 6,
        out_specs=[VMEM, VMEM],
        out_shape=[shape((QUARTER, 2 * all_slots), bf16), shape((2 * all_slots, QUARTER), bf16)],
        compiler_params=params(16),
        cost_estimate=cost(6e6, 5e6),
        name="table",
    )(rows_cos[:LANES], rows_sin[:LANES], rows_cos[LANES:], rows_sin[LANES:], cols_cos, cols_sin)

    adv, base = pl.pallas_call(
        advect_kernel,
        in_specs=[VMEM] * 6,
        out_specs=[VMEM, VMEM],
        out_shape=[shape((bins, points), f32)] * 2,
        compiler_params=params(24),
        cost_estimate=cost(5e8, 4e6),
        name="advect",
    )(
        wave_state,
        jnp.concatenate([low, high], axis=1),
        edge_source[None, :],
        edge_target[None, :],
        bin_speed[:, None],
        interaction,
    )

    lat_row = cell_index // LON
    rows = cell_index - lat_row * LON
    hot = (lat_row[:, None] == jnp.arange(LANES, dtype=i32)[None, :]).astype(bf16)
    total_points = cell_index.shape[0]
    picked = pl.pallas_call(
        functools.partial(surface_kernel, all_slots),
        in_specs=[VMEM, VMEM, VMEM, SMEM, VMEM],
        out_specs=VMEM,
        out_shape=shape((columns, points), bf16),
        scratch_shapes=[pltpu.VMEM((LON, LANES), f32), pltpu.VMEM((total_points, LANES), f32)],
        compiler_params=params(32),
        cost_estimate=cost(1e9, 4e6),
        name="surface",
    )(gathered, long, wave_slot[:, None], rows, hot)
    forcing = lax.all_to_all(picked, "fld", split_axis=0, concat_axis=0, tiled=True)

    wave_next, stress = pl.pallas_call(
        wave_kernel,
        in_specs=[VMEM] * 5,
        out_specs=[VMEM, VMEM],
        out_shape=[shape((bins, points), bf16), shape((owners, points), f32)],
        compiler_params=params(16),
        cost_estimate=cost(1e7, 2e6, bins * points),
        name="wave",
    )(forcing, coupling_in, adv, base, momentum[:, None])
    stresses = lax.all_to_all(stress, "lat", split_axis=0, concat_axis=0, tiled=True)

    bulk, _ = lax.optimization_barrier((bulk, stress))
    lat_rows = lats // owners
    row_cells = lat_rows * LON
    mixed_rows, place_high, place_hot = pl.pallas_call(
        functools.partial(synthesis_kernel, all_slots, levels),
        in_specs=[VMEM, VMEM, VMEM, SMEM],
        out_specs=[VMEM, VMEM, VMEM],
        out_shape=[
            shape((lat_rows, levels, LON), f32),
            shape((owners, points), i32),
            shape((LANES, owners * points), bf16),
        ],
        scratch_shapes=[
            pltpu.VMEM((owners * 32, LANES), f32),
            pltpu.VMEM((owners * 8, LANES), f32),
            pltpu.VMEM((640, 2 * all_slots), bf16),
        ],
        compiler_params=params(32),
        cost_estimate=cost(1.2e9, 6e6),
        name="synthesis",
    )(bulk, wave_slot[None, :], wide, (lat * row_cells)[None])

    partial = pl.pallas_call(
        scatter_kernel,
        in_specs=[VMEM] * 3,
        out_specs=VMEM,
        out_shape=shape((columns, row_cells // LANES, LANES), bf16),
        compiler_params=params(16),
        cost_estimate=cost(1e8, 2e6),
        name="scatter",
    )(stresses, place_high, place_hot)
    partials = lax.all_to_all(partial, "fld", split_axis=0, concat_axis=0, tiled=True)

    mixed = pl.pallas_call(
        final_kernel,
        in_specs=[VMEM, VMEM, VMEM, SMEM],
        out_specs=VMEM,
        out_shape=shape((lat_rows, 1, levels, LON), bf16),
        compiler_params=params(16),
        cost_estimate=cost(1e6, 3e6),
        name="final",
    )(mixed_rows, partials, column, surface_drag)
    return (mixed, wave_next)


def solution(mesh):
    in_specs = (
        P("lat", None, "fld", None, None),
        P("lat", None, None),
        P(),
        P(),
        P(),
        P(),
        P(),
        P(None, ("lat", "fld")),
        P("lat"),
        P(("lat", "fld")),
        P(("lat", "fld")),
        P("fld"),
        P(),
    )
    out_specs = (P("lat", "fld", None, None), P(None, ("lat", "fld")))
    return jax.shard_map(local, mesh=mesh, in_specs=in_specs, out_specs=out_specs, check_vma=False)
```

```python
import functools

import jax
import jax.numpy as jnp
from jax import lax
from jax.experimental import pallas as pl
from jax.experimental.pallas import tpu as pltpu
from jax.sharding import PartitionSpec as P

LON = 2560
RIM = 64
QUARTER = LON // 4
LANES = 128

time_step = 0.25

bf16 = jnp.bfloat16
f32 = jnp.float32
i32 = jnp.int32

NN = (((1,), (0,)), ((), ()))
NT = (((1,), (1,)), ((), ()))

VMEM = pl.BlockSpec(memory_space=pltpu.VMEM)
SMEM = pl.BlockSpec(memory_space=pltpu.SMEM)


def dot(a, b, dims=NN):
    return lax.dot_general(a, b, dims, preferred_element_type=f32)


def after(value, other):
    return lax.optimization_barrier((value, other))[0]


def lane_of(shape):
    return lax.broadcasted_iota(i32, shape, len(shape) - 1)


def params(mib, **more):
    return pltpu.CompilerParams(vmem_limit_bytes=mib << 20, **more)


def cost(flops, nbytes, trans=0):
    return pl.CostEstimate(flops=int(flops), bytes_accessed=int(nbytes), transcendentals=int(trans))


def legendre_kernel(per, slots, wave_ref, leg_ref, spec_ref, f0_ref, f1_ref, x_ref, s0, s1, low):
    step = pl.program_id(0)
    lats, degrees = leg_ref.shape[1:]
    levels = f0_ref.shape[1]

    @pl.when(step == 0)
    def _():
        low[...] = jnp.zeros_like(low)

    column = lane_of((1, degrees))
    lane = lane_of((lats, LANES))
    fill = jnp.zeros((lats, LANES - levels), f32)
    first = lax.axis_index("lat") * slots
    picked = low[0:lats, :]
    for k in range(per):
        slot = step * per + k
        limit = degrees - lax.div(wave_ref[first + slot] * degrees, wave_ref.shape[0])
        weights = jnp.where(column < limit, leg_ref[k].astype(f32), 0.0).astype(bf16)
        for c, store in ((0, s0), (1, s1)):
            sums = dot(weights, spec_ref[k, c, 0], NT)
            store[pl.ds(slot, lats, stride=slots), :] = jnp.concatenate([sums, fill], axis=1)
            lowest = jnp.broadcast_to(sums[:, levels - 1 : levels], (lats, LANES))
            picked = jnp.where(lane == c * slots + slot, lowest, picked)
    low[0:lats, :] = picked

    @pl.when(step == pl.num_programs(0) - 1)
    def _():
        f0_ref[...] = s0[:, 0:levels].astype(bf16)
        f1_ref[...] = s1[:, 0:levels].astype(bf16)
        turned = low[...].T
        tail = turned[24:32, :]
        lane8 = lane_of((8, LANES))
        rows = [
            jnp.where(lane8 < 96, turned[8 * h : 8 * h + 8, :], pltpu.roll(tail, 96 - 32 * h, 1))
            for h in range(3)
        ]
        packed = jnp.concatenate(rows, axis=0).astype(bf16)
        x_ref[...] = jnp.broadcast_to(packed[None], x_ref.shape)


def inverse_kernel(levels, mix_ref, w_ref, col_ref, left, right):
    width = 2 * LANES
    lane = lax.broadcasted_iota(i32, (2, width), 1)
    start = lax.broadcasted_iota(i32, (2, width), 0) * levels
    unit = lane - start
    ratio, part = [], []
    for level in range(levels):
        below = jnp.full((2, width), mix_ref[level], f32)
        rhs = (unit == level).astype(f32)
        if level == 0:
            scale = 1.0 / (1.0 + below)
            part.append(rhs * scale)
        else:
            above = jnp.full((2, width), mix_ref[level - 1], f32)
            scale = 1.0 / (1.0 + below + above - above * ratio[-1])
            part.append((rhs + above * part[-1]) * scale)
        ratio.append(below * scale)
    solved = part[-1]
    for level in range(levels - 1, -1, -1):
        if level < levels - 1:
            solved = part[level] + ratio[level] * solved
        left[2 * level : 2 * level + 2, :] = solved[:, :LANES]
        right[2 * level : 2 * level + 2, :] = solved[:, LANES:]
    for c in range(2):
        block = jnp.concatenate([half[pl.ds(c, levels, stride=2), :] for half in (left, right)], axis=1)
        high = block.astype(bf16)
        w_ref[2 * c] = high
        w_ref[2 * c + 1] = (block - high.astype(f32)).astype(bf16)
        if c == 0:
            col_ref[...] = jnp.broadcast_to(block[:, levels - 1 : levels], col_ref.shape)


def mix_kernel(owners, f0_ref, f1_ref, w_ref, codes_ref, main_ref, tail_ref, rest):
    sums = dot(f0_ref[...], w_ref[0]) + dot(f0_ref[...], w_ref[1])
    sums += dot(f1_ref[...], w_ref[2]) + dot(f1_ref[...], w_ref[3])
    count = sums.shape[0]
    rest[...] = sums[:, LANES:]
    lane = lane_of((count // 4, LANES))
    tail = jnp.broadcast_to(codes_ref[...][None], (owners, 8, LANES)).reshape(count // 4, LANES)
    for g in range(4):
        piece = rest[pl.ds(g, count // 4, stride=4), :]
        if g:
            piece = pltpu.roll(piece, 16 * g, 1)
        tail = jnp.where((lane >= 16 * g) & (lane < 16 * g + 16), piece, tail)
    main_ref[...] = sums[:, :LANES].reshape(owners, count // owners, LANES).astype(bf16)
    tail_ref[...] = tail.reshape(owners, 8, LANES)


def waves(wave_ref):
    slots = wave_ref.shape[1]
    wave = wave_ref[...].astype(f32)

    def angles(count, unit):
        step = lax.broadcasted_iota(i32, (count, slots), 0).astype(f32) * float(unit)
        turn = step * wave
        turn = turn - float(LON) * jnp.floor(turn * (1.0 / LON) + 0.5)
        phase = turn * (2.0 * jnp.pi / LON)
        return jnp.cos(phase), jnp.sin(phase)

    ones = angles(16, 1)
    tens = angles(8, 16)
    parts = [added((tens[0][k : k + 1], tens[1][k : k + 1]), ones) for k in range(8)]
    return [jnp.concatenate([p[c] for p in parts], axis=0) for c in range(2)], angles(8, LANES)


def added(a, b):
    return a[0] * b[0] - a[1] * b[1], a[1] * b[0] + a[0] * b[1]


def long_kernel(wave_ref, long_ref):
    slots = wave_ref.shape[1]
    fine, coarse = waves(wave_ref)
    for a in range(QUARTER // LANES):
        c, s = added((coarse[0][a : a + 1], coarse[1][a : a + 1]), fine)
        rows = slice(a * LANES, (a + 1) * LANES)
        long_ref[rows, 0:slots] = c.astype(bf16)
        long_ref[rows, slots : 2 * slots] = (-s).astype(bf16)


def wide_kernel(wave_ref, wide_ref):
    slots = wave_ref.shape[1]
    fine, coarse = waves(wave_ref)
    for first in range(0, slots, LANES):
        mine = slice(first, first + LANES)
        turned = [x[:, mine].T for x in fine]
        for a in range(QUARTER // LANES):
            start = [jnp.broadcast_to(x[a : a + 1, mine], (LANES, LANES)).T for x in coarse]
            c, s = added(start, turned)
            columns = slice(a * LANES, (a + 1) * LANES)
            wide_ref[mine, columns] = c.astype(bf16)
            wide_ref[slots + first : slots + first + LANES, columns] = (-s).astype(bf16)


def turned_pair(first, second, wave, m):
    if m == 0:
        return first, second
    turns = (wave * m) & 3
    even = (turns & 1) == 0
    sign0 = jnp.where((turns == 0) | (turns == 3), 1.0, -1.0)
    sign1 = jnp.where((turns == 0) | (turns == 1), 1.0, -1.0)
    return jnp.where(even, first, second) * sign0, jnp.where(even, second, first) * sign1


def unpacked(x_ref):
    peers = x_ref.shape[0]
    x = x_ref[...].astype(f32)
    lane = lane_of((peers, 8, LANES))
    tail = jnp.zeros((peers, 8, LANES), f32)
    for h in range(3):
        moved = pltpu.roll(x[:, 8 * h : 8 * h + 8, :].reshape(peers * 8, LANES), 32 + 32 * h, 1)
        tail = jnp.where((lane >= 32 * h) & (lane < 32 * h + 32), moved.reshape(peers, 8, LANES), tail)
    return x[:, 0:16, :], jnp.concatenate([x[:, 16:24, :], tail], axis=1)


def surface_kernel(slots, own_ref, other_ref, long_ref, wave_ref, row_ref, lat_ref, o_ref, surface, picked):
    first = lax.rem(lax.axis_index("lat"), 2) == 0
    own, other = unpacked(own_ref), unpacked(other_ref)
    real, imaginary = [
        jnp.stack([jnp.where(first, a, b), jnp.where(first, b, a)], axis=1).reshape(slots, LANES)
        for a, b in zip(own, other)
    ]
    wave = upright(wave_ref).astype(i32)
    pairs = [turned_pair(real, imaginary, wave, m) for m in range(4)]
    coefficients = jnp.concatenate(
        [jnp.concatenate([p[c].astype(bf16) for p in pairs], axis=1) for c in range(2)], axis=0
    )
    values = dot(long_ref[...], coefficients).astype(bf16).astype(f32)
    for m in range(4):
        surface[m * QUARTER : (m + 1) * QUARTER, :] = values[:, m * LANES : (m + 1) * LANES]

    def fetch(block, carry):
        for u in range(32):
            p = block * 32 + u
            picked[pl.ds(p, 1), :] = surface[pl.ds(row_ref[p], 1), :]
        return carry

    lax.fori_loop(0, picked.shape[0] // 32, fetch, 0)
    row = lax.broadcasted_iota(i32, (LANES, LANES), 0)
    diagonal = row == lane_of((LANES, LANES))
    for k in range(lat_ref.shape[0]):
        mine = slice(k * LANES, (k + 1) * LANES)
        hot = (row == lat_ref[k : k + 1, :]).astype(f32).astype(bf16)
        product = dot(picked[mine, :].astype(bf16), hot)
        o_ref[k : k + 1, :] = jnp.sum(jnp.where(diagonal, product, 0.0), axis=0, keepdims=True)


def upright(row_ref):
    count = row_ref.shape[1]
    parts = []
    for first in range(0, count, LANES):
        size = min(LANES, count - first)
        part = row_ref[:, first : first + size]
        if size < LANES:
            part = jnp.concatenate([part, jnp.zeros((1, LANES - size), f32)], axis=1)
        parts.append(jnp.broadcast_to(part, (LANES, LANES)).T[0:size])
    return jnp.concatenate(parts, axis=0)


def advect_kernel(
    state_ref, low_ref, high_ref, source_ref, target_ref, speed_ref, inter_ref, adv_ref, base_ref, held, sem
):
    fetch = pltpu.make_async_copy(inter_ref, held, sem)
    fetch.start()
    edges = source_ref.shape[1]
    points = state_ref.shape[1]
    source_hot = (lax.broadcasted_iota(i32, (points + 2 * RIM, edges), 0) == source_ref[...]).astype(f32)
    target_hot = (lax.broadcasted_iota(i32, (points, edges), 0) == target_ref[...]).astype(f32)
    source_hot, target_hot = source_hot.astype(bf16), target_hot.astype(bf16)
    routes = dot(source_hot, target_hot, NT)
    counts = dot(jnp.ones((8, edges), bf16), target_hot, NT)[0:1, :]
    none = jnp.zeros((points - RIM, points), f32)
    tables = (
        (low_ref, jnp.concatenate([none, routes[0:RIM]], axis=0)),
        (state_ref, routes[RIM : RIM + points]),
        (high_ref, jnp.concatenate([routes[RIM + points :], none], axis=0)),
    )
    inflow = None
    for values, table in tables:
        high = table.astype(bf16)
        rest = (table - high.astype(f32)).astype(bf16)
        part = dot(values[...], high) + dot(values[...], rest)
        inflow = part if inflow is None else inflow + part
    current = state_ref[...].astype(f32)
    advected = current + upright(speed_ref) * (inflow - counts * current)
    squared = (advected * advected).astype(bf16)
    fetch.wait()
    transfer = dot(held[...], squared)
    adv_ref[...] = time_step * advected
    base_ref[...] = advected + time_step * transfer


def wave_kernel(forcing_ref, coupling_ref, adv_ref, base_ref, momentum_ref, main_ref, tail_ref, next_ref, o_ref):
    growth = jnp.tanh(dot(coupling_ref[...], forcing_ref[...].astype(bf16)))
    wave_new = base_ref[...] + growth * adv_ref[...]
    next_ref[...] = wave_new.astype(bf16)
    stress = jnp.sum(upright(momentum_ref) * growth * wave_new, axis=0, keepdims=True)
    stress = jnp.broadcast_to(stress, (8, LANES))
    high = stress.astype(bf16).astype(f32)
    low = stress - high
    row = lax.broadcasted_iota(i32, (8, LANES), 0)
    lane = lane_of((8, LANES))
    part = jnp.where(row < 6, high, low)
    part = jnp.where((row & 1) == 0, pltpu.roll(part, 64, 1), part)
    joined = jnp.where(((row >= 4) & (lane >= 64))[None], part[None], tail_ref[...])
    o_ref[...] = jnp.concatenate([main_ref[...].astype(f32), joined], axis=1).astype(bf16)


def synthesis_kernel(slots, y_ref, wave_ref, wide_ref, d_ref, rest, lhs):
    levels = d_ref.shape[1]
    peers = y_ref.shape[0]
    y = y_ref[...].astype(f32)
    main = y[:, 0:32, :]
    tail = y[:, 32:40, :].reshape(peers * 8, LANES)
    for g in range(4):
        rest[pl.ds(g, peers * 8, stride=4), :] = pltpu.roll(tail, LANES - 16 * g, 1) if g else tail
    wave = wave_ref[...]
    others = rest[...].reshape(peers, 32, LANES)
    padded = 80
    fill = jnp.zeros((padded - levels, slots), f32)
    for t in range(2):
        a = main[:, 16 * t : 16 * t + 16, :].reshape(slots, LANES).T
        b = others[:, 16 * t : 16 * t + 16, :].reshape(slots, LANES).T
        first = a[0:levels]
        second = jnp.concatenate([a[levels:], b[0 : 2 * levels - LANES]], axis=0)
        for m in range(4):
            p, q = turned_pair(first, second, wave, m)
            rows = slice((t * 4 + m) * padded, (t * 4 + m + 1) * padded)
            lhs[rows, 0:slots] = jnp.concatenate([p, fill], axis=0).astype(bf16)
            lhs[rows, slots : 2 * slots] = jnp.concatenate([q, fill], axis=0).astype(bf16)
    for t in range(2):
        sums = dot(lhs[t * 4 * padded : (t + 1) * 4 * padded, :], wide_ref[...])
        for m in range(4):
            d_ref[t, :, m * QUARTER : (m + 1) * QUARTER] = sums[m * padded : m * padded + levels].astype(bf16)


def scatter_kernel(y_ref, o_ref, tails):
    peers = y_ref.shape[0]
    height = o_ref.shape[1]
    tails[...] = y_ref[...].astype(f32)[:, 32:40, :].reshape(peers * 8, LANES)
    lane = lane_of((peers, LANES))

    def line(k):
        left = pltpu.roll(tails[pl.ds(2 * k, peers, stride=8), :], 64, 1)
        return jnp.where(lane < 64, left, tails[pl.ds(2 * k + 1, peers, stride=8), :])

    v0, v1, high, low = [line(k) for k in range(4)]
    cell = (jnp.abs(v0) - 1.0) + 256.0 * (jnp.abs(v1) - 1.0)
    cell += jnp.where(v0 < 0, 65536.0, 0.0) + jnp.where(v1 < 0, 131072.0, 0.0)
    cell = cell.astype(i32) - lax.axis_index("lat") * (height * LANES)
    upper = cell >> 7
    at = cell & (LANES - 1)
    row = lax.broadcasted_iota(i32, (LANES, LANES), 0)
    sums = None
    for k in range(peers):
        one = slice(k, k + 1)
        inside = row[0:height] == upper[one]
        spread = jnp.concatenate([jnp.where(inside, high[one], 0.0), jnp.where(inside, low[one], 0.0)], axis=0)
        hot = (row == at[one]).astype(f32).astype(bf16)
        both = (spread.astype(bf16), hot)
        sums = [both] if sums is None else sums + [both]
    spread = jnp.concatenate([p[0] for p in sums], axis=1)
    hot = jnp.concatenate([p[1] for p in sums], axis=1)
    total = dot(spread, hot, NT)
    o_ref[...] = jnp.broadcast_to((total[0:height] + total[height:]).astype(bf16)[None], o_ref.shape)


def final_kernel(d_ref, part_ref, col_ref, drag_ref, o_ref):
    stress = jnp.sum(part_ref[...].astype(f32), axis=0)
    push = col_ref[...] * drag_ref[0]
    chunks = LON // LANES
    for t in range(2):
        for k in range(chunks):
            columns = slice(k * LANES, (k + 1) * LANES)
            line = stress[t * chunks + k : t * chunks + k + 1, :]
            o_ref[t, 0, :, columns] = (d_ref[t, :, columns].astype(f32) + push * line).astype(bf16)


def local(
    spectral,
    legendre,
    wave_slot,
    coupling_in,
    interaction,
    bin_speed,
    momentum,
    wave_state,
    cell_index,
    edge_source,
    edge_target,
    surface_drag,
    mixing,
):
    slots, _, _, levels, degrees = spectral.shape
    lats = legendre.shape[1]
    all_slots = wave_slot.shape[0]
    owners = lax.axis_size("lat")
    columns = lax.axis_size("fld")
    bins, points = wave_state.shape
    fld = lax.axis_index("fld")
    shape = jax.ShapeDtypeStruct

    per = 4
    wave_row = wave_slot[None, :]
    f0, f1, packed = pl.pallas_call(
        functools.partial(legendre_kernel, per, slots),
        grid=(slots // per,),
        in_specs=[
            SMEM,
            pl.BlockSpec((per, lats, degrees), lambda i: (i, 0, 0)),
            pl.BlockSpec((per, 2, 1, levels, degrees), lambda i: (i, 0, 0, 0, 0)),
        ],
        out_specs=[
            pl.BlockSpec((lats * slots, levels), lambda i: (0, 0)),
            pl.BlockSpec((lats * slots, levels), lambda i: (0, 0)),
            pl.BlockSpec((owners // 2, 24, LANES), lambda i: (0, 0, 0)),
        ],
        out_shape=[
            shape((lats * slots, levels), bf16),
            shape((lats * slots, levels), bf16),
            shape((owners // 2, 24, LANES), bf16),
        ],
        scratch_shapes=[
            pltpu.VMEM((lats * slots, LANES), f32),
            pltpu.VMEM((lats * slots, LANES), f32),
            pltpu.VMEM((LANES, LANES), f32),
        ],
        compiler_params=params(53),
        cost_estimate=cost(3e8, 5e6),
        name="legendre",
    )(wave_slot, legendre, spectral)
    same_core = [[2 * k + core for k in range(owners // 2)] for core in range(2)]
    own_part = lax.all_to_all(
        packed, "lat", split_axis=0, concat_axis=0, tiled=True, axis_index_groups=same_core
    )
    other_part = lax.ppermute(own_part, "lat", [(k, k ^ 1) for k in range(owners)])
    long = pl.pallas_call(
        long_kernel,
        in_specs=[VMEM],
        out_specs=VMEM,
        out_shape=shape((QUARTER, 2 * all_slots), bf16),
        compiler_params=params(10),
        cost_estimate=cost(6e6, 3e6),
        name="long",
    )(after(wave_row, own_part))

    tiles = owners * columns
    up = [(k, k + 1) for k in range(tiles - 1)]
    low = lax.ppermute(wave_state, ("lat", "fld"), up)
    high = lax.ppermute(wave_state, ("lat", "fld"), [(b, a) for a, b in up])

    lat_row = cell_index // LON
    rows = cell_index - lat_row * LON
    picked = pl.pallas_call(
        functools.partial(surface_kernel, all_slots),
        in_specs=[VMEM, VMEM, VMEM, VMEM, SMEM, VMEM],
        out_specs=VMEM,
        out_shape=shape((columns, points), f32),
        scratch_shapes=[pltpu.VMEM((LON, LANES), f32), pltpu.VMEM((columns * points, LANES), f32)],
        compiler_params=params(14),
        cost_estimate=cost(1e9, 4e6),
        name="surface",
    )(own_part, other_part, long, wave_row.astype(f32), rows, lat_row.reshape(columns, points))
    forcing = lax.all_to_all(picked, "fld", split_axis=0, concat_axis=0, tiled=True)

    mixers, column = pl.pallas_call(
        functools.partial(inverse_kernel, levels),
        in_specs=[SMEM],
        out_specs=[VMEM, VMEM],
        out_shape=[shape((4, levels, 2 * LANES), bf16), shape((levels, LANES), f32)],
        scratch_shapes=[pltpu.VMEM((2 * levels, LANES), f32)] * 2,
        compiler_params=params(4),
        cost_estimate=cost(3e6, 2e5),
        name="inverse",
    )(mixing)
    own_cells = lax.dynamic_slice_in_dim(cell_index, fld * points, points)
    sign0 = 1 - 2 * ((own_cells >> 16) & 1)
    sign1 = 1 - 2 * (own_cells >> 17)
    codes = jnp.stack([((own_cells & 255) + 1) * sign0, (((own_cells >> 8) & 255) + 1) * sign1])
    codes = jnp.pad(codes.astype(f32).reshape(4, 64), ((0, 4), (64, 0)))
    main, tail = pl.pallas_call(
        functools.partial(mix_kernel, owners),
        in_specs=[VMEM] * 4,
        out_specs=[VMEM, VMEM],
        out_shape=[shape((owners, 32, LANES), bf16), shape((owners, 8, LANES), f32)],
        scratch_shapes=[pltpu.VMEM((lats * slots, LANES), f32)],
        compiler_params=params(10),
        cost_estimate=cost(2e8, 2e6),
        name="mix",
    )(f0, f1, mixers, codes)

    adv, base = pl.pallas_call(
        advect_kernel,
        in_specs=[VMEM] * 6 + [pl.BlockSpec(memory_space=pl.ANY)],
        out_specs=[VMEM] * 2,
        out_shape=[shape((bins, points), f32)] * 2,
        scratch_shapes=[pltpu.VMEM((bins, bins), bf16), pltpu.SemaphoreType.DMA],
        compiler_params=params(51),
        cost_estimate=cost(5e8, 4e6),
        name="advect",
    )(
        wave_state,
        low,
        high,
        after(edge_source[None, :], picked),
        edge_target[None, :],
        bin_speed[None, :],
        interaction,
    )

    wave_next, outgoing = pl.pallas_call(
        wave_kernel,
        in_specs=[VMEM] * 7,
        out_specs=[VMEM, VMEM],
        out_shape=[shape((bins, points), bf16), shape((owners, 40, LANES), bf16)],
        compiler_params=params(8),
        cost_estimate=cost(1e7, 2e6, bins * points),
        name="wave",
    )(forcing, coupling_in, adv, base, momentum[None, :], main, tail)
    bulk = lax.all_to_all(outgoing, "lat", split_axis=0, concat_axis=0, tiled=True)

    lat_rows = lats // owners
    partial = pl.pallas_call(
        scatter_kernel,
        in_specs=[VMEM],
        out_specs=VMEM,
        out_shape=shape((columns, lat_rows * LON // LANES, LANES), bf16),
        scratch_shapes=[pltpu.VMEM((owners * 8, LANES), f32)],
        compiler_params=params(8),
        cost_estimate=cost(1e8, 2e6),
        name="scatter",
    )(bulk)
    partials = lax.all_to_all(partial, "fld", split_axis=0, concat_axis=0, tiled=True)

    bulk = after(bulk, partial)
    wide = pl.pallas_call(
        wide_kernel,
        in_specs=[VMEM],
        out_specs=VMEM,
        out_shape=shape((2 * all_slots, QUARTER), bf16),
        compiler_params=params(10),
        cost_estimate=cost(6e6, 3e6),
        name="wide",
    )(after(wave_row, partial))
    mixed_rows = pl.pallas_call(
        functools.partial(synthesis_kernel, all_slots),
        in_specs=[VMEM, VMEM, VMEM],
        out_specs=VMEM,
        out_shape=shape((lat_rows, levels, LON), bf16),
        scratch_shapes=[pltpu.VMEM((owners * 32, LANES), f32), pltpu.VMEM((640, 2 * all_slots), bf16)],
        compiler_params=params(14),
        cost_estimate=cost(1.2e9, 6e6),
        name="synthesis",
    )(bulk, wave_row, wide)

    mixed = pl.pallas_call(
        final_kernel,
        in_specs=[VMEM, VMEM, VMEM, SMEM],
        out_specs=VMEM,
        out_shape=shape((lat_rows, 1, levels, LON), bf16),
        compiler_params=params(6),
        cost_estimate=cost(1e6, 3e6),
        name="final",
    )(mixed_rows, partials, column, surface_drag)
    return (mixed, wave_next)


def solution(mesh):
    in_specs = (
        P("lat", None, "fld", None, None),
        P("lat", None, None),
        P(),
        P(),
        P(),
        P(),
        P(),
        P(None, ("lat", "fld")),
        P("lat"),
        P(("lat", "fld")),
        P(("lat", "fld")),
        P("fld"),
        P(),
    )
    out_specs = (P("lat", "fld", None, None), P(None, ("lat", "fld")))
    return jax.shard_map(local, mesh=mesh, in_specs=in_specs, out_specs=out_specs, check_vma=False)
```

```python
import functools

import jax
import jax.numpy as jnp
from jax import lax
from jax.experimental import pallas as pl
from jax.experimental.pallas import tpu as pltpu
from jax.sharding import PartitionSpec as P

LON = 2560
RIM = 64
QUARTER = LON // 4
LANES = 128

time_step = 0.25

bf16 = jnp.bfloat16
f32 = jnp.float32
i32 = jnp.int32

NN = (((1,), (0,)), ((), ()))
NT = (((1,), (1,)), ((), ()))

VMEM = pl.BlockSpec(memory_space=pltpu.VMEM)
SMEM = pl.BlockSpec(memory_space=pltpu.SMEM)


def dot(a, b, dims=NN):
    return lax.dot_general(a, b, dims, preferred_element_type=f32)


def after(value, other):
    return lax.optimization_barrier((value, other))[0]


def lane_of(shape):
    return lax.broadcasted_iota(i32, shape, len(shape) - 1)


def params(mib, **more):
    return pltpu.CompilerParams(vmem_limit_bytes=mib << 20, **more)


def cost(flops, nbytes, trans=0):
    return pl.CostEstimate(flops=int(flops), bytes_accessed=int(nbytes), transcendentals=int(trans))


def legendre_kernel(per, slots, wave_ref, leg_ref, spec_ref, f_ref, x_ref, s0, s1, low):
    step = pl.program_id(0)
    lats, degrees = leg_ref.shape[1:]
    both = f_ref.shape[1]
    levels = both // 2

    @pl.when(step == 0)
    def _():
        low[...] = jnp.zeros_like(low)

    column = lane_of((1, degrees))
    lane = lane_of((lats, LANES))
    fill = jnp.zeros((lats, 2 * LANES - both), f32)
    first = lax.axis_index("lat") * slots
    picked = low[0:lats, :]
    for k in range(per):
        slot = step * per + k
        limit = degrees - lax.div(wave_ref[first + slot] * degrees, wave_ref.shape[0])
        weights = jnp.where(column < limit, leg_ref[k].astype(f32), 0.0).astype(bf16)
        sums = dot(weights, spec_ref[k], NT)
        s0[pl.ds(slot, lats, stride=slots), :] = sums[:, 0:LANES]
        s1[pl.ds(slot, lats, stride=slots), :] = jnp.concatenate([sums[:, LANES:], fill], axis=1)
        for c in range(2):
            lowest = jnp.broadcast_to(sums[:, (c + 1) * levels - 1 : (c + 1) * levels], (lats, LANES))
            picked = jnp.where(lane == c * slots + slot, lowest, picked)
    low[0:lats, :] = picked

    @pl.when(step == pl.num_programs(0) - 1)
    def _():
        f_ref[...] = jnp.concatenate([s0[...], s1[:, 0 : both - LANES]], axis=1).astype(bf16)
        turned = low[...].T
        tail = turned[24:32, :]
        lane8 = lane_of((8, LANES))
        rows = [
            jnp.where(lane8 < 96, turned[8 * h : 8 * h + 8, :], pltpu.roll(tail, 96 - 32 * h, 1))
            for h in range(3)
        ]
        packed = jnp.concatenate(rows, axis=0).astype(bf16)
        x_ref[...] = jnp.broadcast_to(packed[None], x_ref.shape)


def inverse(levels, mix_ref, col_ref, left, right):
    width = 2 * LANES
    lane = lax.broadcasted_iota(i32, (2, width), 1)
    start = lax.broadcasted_iota(i32, (2, width), 0) * levels
    unit = lane - start
    ratio, part = [], []
    for level in range(levels):
        below = jnp.full((2, width), mix_ref[level], f32)
        rhs = (unit == level).astype(f32)
        if level == 0:
            scale = 1.0 / (1.0 + below)
            part.append(rhs * scale)
        else:
            above = jnp.full((2, width), mix_ref[level - 1], f32)
            scale = 1.0 / (1.0 + below + above - above * ratio[-1])
            part.append((rhs + above * part[-1]) * scale)
        ratio.append(below * scale)
    solved = part[-1]
    for level in range(levels - 1, -1, -1):
        if level < levels - 1:
            solved = part[level] + ratio[level] * solved
        left[2 * level : 2 * level + 2, :] = solved[:, :LANES]
        right[2 * level : 2 * level + 2, :] = solved[:, LANES:]
    blocks = [
        jnp.concatenate([half[pl.ds(c, levels, stride=2), :] for half in (left, right)], axis=1) for c in range(2)
    ]
    col_ref[...] = jnp.broadcast_to(blocks[0][:, levels - 1 : levels], col_ref.shape)
    return jnp.concatenate(blocks, axis=0)


def mix_kernel(owners, mix_ref, f_ref, codes_ref, main_ref, tail_ref, col_ref, rest, left, right):
    mixer = inverse(f_ref.shape[1] // 2, mix_ref, col_ref, left, right)
    high = mixer.astype(bf16)
    sums = dot(f_ref[...], high) + dot(f_ref[...], (mixer - high.astype(f32)).astype(bf16))
    count = sums.shape[0]
    rest[...] = sums[:, LANES:]
    lane = lane_of((count // 4, LANES))
    tail = jnp.broadcast_to(codes_ref[...][None], (owners, 8, LANES)).reshape(count // 4, LANES)
    for g in range(4):
        piece = rest[pl.ds(g, count // 4, stride=4), :]
        if g:
            piece = pltpu.roll(piece, 16 * g, 1)
        tail = jnp.where((lane >= 16 * g) & (lane < 16 * g + 16), piece, tail)
    main_ref[...] = sums[:, :LANES].reshape(owners, count // owners, LANES).astype(bf16)
    tail_ref[...] = tail.reshape(owners, 8, LANES)


def waves(wave_ref):
    slots = wave_ref.shape[1]
    wave = wave_ref[...].astype(f32)

    def angles(count, unit):
        step = lax.broadcasted_iota(i32, (count, slots), 0).astype(f32) * float(unit)
        turn = step * wave
        turn = turn - float(LON) * jnp.floor(turn * (1.0 / LON) + 0.5)
        phase = turn * (2.0 * jnp.pi / LON)
        return jnp.cos(phase), jnp.sin(phase)

    ones = angles(16, 1)
    tens = angles(8, 16)
    parts = [added((tens[0][k : k + 1], tens[1][k : k + 1]), ones) for k in range(8)]
    return [jnp.concatenate([p[c] for p in parts], axis=0) for c in range(2)], angles(8, LANES)


def added(a, b):
    return a[0] * b[0] - a[1] * b[1], a[1] * b[0] + a[0] * b[1]


def long_kernel(wave_ref, long_ref):
    slots = wave_ref.shape[1]
    fine, coarse = waves(wave_ref)
    for a in range(QUARTER // LANES):
        c, s = added((coarse[0][a : a + 1], coarse[1][a : a + 1]), fine)
        rows = slice(a * LANES, (a + 1) * LANES)
        long_ref[rows, 0:slots] = c.astype(bf16)
        long_ref[rows, slots : 2 * slots] = (-s).astype(bf16)


def wide_kernel(wave_ref, wide_ref):
    slots = wave_ref.shape[1]
    fine, coarse = waves(wave_ref)
    for first in range(0, slots, LANES):
        mine = slice(first, first + LANES)
        turned = [x[:, mine].T for x in fine]
        for a in range(QUARTER // LANES):
            start = [jnp.broadcast_to(x[a : a + 1, mine], (LANES, LANES)).T for x in coarse]
            c, s = added(start, turned)
            columns = slice(a * LANES, (a + 1) * LANES)
            wide_ref[mine, columns] = c.astype(bf16)
            wide_ref[slots + first : slots + first + LANES, columns] = (-s).astype(bf16)


def quarters(wave):
    turns = wave & 3
    cos = jnp.where(turns == 0, 1.0, jnp.where(turns == 2, -1.0, 0.0))
    sin = jnp.where(turns == 1, 1.0, jnp.where(turns == 3, -1.0, 0.0))
    return cos, sin, jnp.where((turns & 1) == 0, 1.0, -1.0)


def turned(first, second, quarter):
    cos, sin, half = quarter
    fc, fs, sc, ss = first * cos, first * sin, second * cos, second * sin
    return [(first, second), (fc - ss, fs + sc), (first * half, second * half), (fc + ss, sc - fs)]


def unpacked(x_ref):
    peers = x_ref.shape[0]
    x = x_ref[...].astype(f32)
    lane = lane_of((peers, 8, LANES))
    tail = jnp.zeros((peers, 8, LANES), f32)
    for h in range(3):
        moved = pltpu.roll(x[:, 8 * h : 8 * h + 8, :].reshape(peers * 8, LANES), 32 + 32 * h, 1)
        tail = jnp.where((lane >= 32 * h) & (lane < 32 * h + 32), moved.reshape(peers, 8, LANES), tail)
    return x[:, 0:16, :], jnp.concatenate([x[:, 16:24, :], tail], axis=1)


def surface_kernel(slots, own_ref, other_ref, long_ref, wave_ref, row_ref, lat_ref, o_ref, surface, picked):
    first = lax.rem(lax.axis_index("lat"), 2) == 0
    own, other = unpacked(own_ref), unpacked(other_ref)
    real, imaginary = [
        jnp.stack([jnp.where(first, a, b), jnp.where(first, b, a)], axis=1).reshape(slots, LANES)
        for a, b in zip(own, other)
    ]
    pairs = turned(real, imaginary, [upright(x) for x in quarters(wave_ref[...])])
    coefficients = jnp.concatenate(
        [jnp.concatenate([p[c].astype(bf16) for p in pairs], axis=1) for c in range(2)], axis=0
    )
    values = dot(long_ref[...], coefficients).astype(bf16).astype(f32)
    for m in range(4):
        surface[m * QUARTER : (m + 1) * QUARTER, :] = values[:, m * LANES : (m + 1) * LANES]

    def fetch(block, carry):
        start = pl.multiple_of(block * LANES, LANES)
        window = picked.at[pl.ds(start, LANES), :]
        for u in range(LANES):
            window[u : u + 1, :] = surface[pl.ds(row_ref[start + u], 1), :]
        return carry

    lax.fori_loop(0, picked.shape[0] // LANES, fetch, 0)
    row = lax.broadcasted_iota(i32, (LANES, LANES), 0)
    diagonal = row == lane_of((LANES, LANES))
    for k in range(lat_ref.shape[0]):
        mine = slice(k * LANES, (k + 1) * LANES)
        hot = (row == lat_ref[k : k + 1, :]).astype(f32).astype(bf16)
        product = dot(picked[mine, :].astype(bf16), hot)
        o_ref[k : k + 1, :] = jnp.sum(jnp.where(diagonal, product, 0.0), axis=0, keepdims=True)


def upright(row_ref):
    row = row_ref[...]
    count = row.shape[1]
    parts = []
    for first in range(0, count, LANES):
        size = min(LANES, count - first)
        part = row[:, first : first + size]
        if size < LANES:
            part = jnp.concatenate([part, jnp.zeros((1, LANES - size), f32)], axis=1)
        parts.append(jnp.broadcast_to(part, (LANES, LANES)).T[0:size])
    return jnp.concatenate(parts, axis=0)


def advect_kernel(
    state_ref, low_ref, high_ref, source_ref, target_ref, speed_ref, inter_ref, adv_ref, base_ref, held, sem
):
    fetch = pltpu.make_async_copy(inter_ref, held, sem)
    fetch.start()
    edges = source_ref.shape[1]
    points = state_ref.shape[1]
    source_hot = (lax.broadcasted_iota(i32, (points + 2 * RIM, edges), 0) == source_ref[...]).astype(f32)
    target_hot = (lax.broadcasted_iota(i32, (points, edges), 0) == target_ref[...]).astype(f32)
    source_hot, target_hot = source_hot.astype(bf16), target_hot.astype(bf16)
    routes = dot(source_hot, target_hot, NT)
    counts = dot(jnp.ones((8, edges), bf16), target_hot, NT)[0:1, :]
    none = jnp.zeros((points - RIM, points), f32)
    tables = (
        (low_ref, jnp.concatenate([none, routes[0:RIM]], axis=0)),
        (state_ref, routes[RIM : RIM + points]),
        (high_ref, jnp.concatenate([routes[RIM + points :], none], axis=0)),
    )
    inflow = None
    for values, table in tables:
        high = table.astype(bf16)
        rest = (table - high.astype(f32)).astype(bf16)
        part = dot(values[...], high) + dot(values[...], rest)
        inflow = part if inflow is None else inflow + part
    current = state_ref[...].astype(f32)
    advected = current + upright(speed_ref) * (inflow - counts * current)
    squared = (advected * advected).astype(bf16)
    fetch.wait()
    transfer = dot(held[...], squared)
    adv_ref[...] = time_step * advected
    base_ref[...] = advected + time_step * transfer


def wave_kernel(forcing_ref, coupling_ref, adv_ref, base_ref, momentum_ref, main_ref, tail_ref, next_ref, o_ref):
    growth = jnp.tanh(dot(coupling_ref[...], forcing_ref[...].astype(bf16)))
    wave_new = base_ref[...] + growth * adv_ref[...]
    next_ref[...] = wave_new.astype(bf16)
    stress = jnp.sum(upright(momentum_ref) * growth * wave_new, axis=0, keepdims=True)
    stress = jnp.broadcast_to(stress, (8, LANES))
    high = stress.astype(bf16).astype(f32)
    low = stress - high
    row = lax.broadcasted_iota(i32, (8, LANES), 0)
    lane = lane_of((8, LANES))
    part = jnp.where(row < 6, high, low)
    part = jnp.where((row & 1) == 0, pltpu.roll(part, 64, 1), part)
    joined = jnp.where(((row >= 4) & (lane >= 64))[None], part[None], tail_ref[...])
    o_ref[...] = jnp.concatenate([main_ref[...].astype(f32), joined], axis=1).astype(bf16)


def synthesis_kernel(slots, y_ref, wave_ref, wide_ref, d_ref, rest, lhs):
    levels = d_ref.shape[1]
    peers = y_ref.shape[0]
    y = y_ref[...].astype(f32)
    main = y[:, 0:32, :]
    tail = y[:, 32:40, :].reshape(peers * 8, LANES)
    for g in range(4):
        rest[pl.ds(g, peers * 8, stride=4), :] = pltpu.roll(tail, LANES - 16 * g, 1) if g else tail
    quarter = quarters(wave_ref[...])
    others = rest[...].reshape(peers, 32, LANES)
    padded = 80
    fill = jnp.zeros((padded - levels, slots), f32)
    for t in range(2):
        a = main[:, 16 * t : 16 * t + 16, :].reshape(slots, LANES).T
        b = others[:, 16 * t : 16 * t + 16, :].reshape(slots, LANES).T
        first = a[0:levels]
        second = jnp.concatenate([a[levels:], b[0 : 2 * levels - LANES]], axis=0)
        for m, (p, q) in enumerate(turned(first, second, quarter)):
            rows = slice((t * 4 + m) * padded, (t * 4 + m + 1) * padded)
            lhs[rows, 0:slots] = jnp.concatenate([p, fill], axis=0).astype(bf16)
            lhs[rows, slots : 2 * slots] = jnp.concatenate([q, fill], axis=0).astype(bf16)
    for t in range(2):
        sums = dot(lhs[t * 4 * padded : (t + 1) * 4 * padded, :], wide_ref[...])
        for m in range(4):
            d_ref[t, :, m * QUARTER : (m + 1) * QUARTER] = sums[m * padded : m * padded + levels].astype(bf16)


def scatter_kernel(y_ref, o_ref, tails):
    peers = y_ref.shape[0]
    height = o_ref.shape[1]
    tails[...] = y_ref[...].astype(f32)[:, 32:40, :].reshape(peers * 8, LANES)
    lane = lane_of((peers, LANES))

    def line(k):
        left = pltpu.roll(tails[pl.ds(2 * k, peers, stride=8), :], 64, 1)
        return jnp.where(lane < 64, left, tails[pl.ds(2 * k + 1, peers, stride=8), :])

    v0, v1, high, low = [line(k) for k in range(4)]
    cell = (jnp.abs(v0) - 1.0) + 256.0 * (jnp.abs(v1) - 1.0)
    cell += jnp.where(v0 < 0, 65536.0, 0.0) + jnp.where(v1 < 0, 131072.0, 0.0)
    cell = cell.astype(i32) - lax.axis_index("lat") * (height * LANES)
    upper = cell >> 7
    at = cell & (LANES - 1)
    row = lax.broadcasted_iota(i32, (LANES, LANES), 0)
    sums = None
    for k in range(peers):
        one = slice(k, k + 1)
        inside = row[0:height] == upper[one]
        spread = jnp.concatenate([jnp.where(inside, high[one], 0.0), jnp.where(inside, low[one], 0.0)], axis=0)
        hot = (row == at[one]).astype(f32).astype(bf16)
        both = (spread.astype(bf16), hot)
        sums = [both] if sums is None else sums + [both]
    spread = jnp.concatenate([p[0] for p in sums], axis=1)
    hot = jnp.concatenate([p[1] for p in sums], axis=1)
    total = dot(spread, hot, NT)
    o_ref[...] = jnp.broadcast_to((total[0:height] + total[height:]).astype(bf16)[None], o_ref.shape)


def final_kernel(d_ref, part_ref, col_ref, drag_ref, o_ref):
    stress = jnp.sum(part_ref[...].astype(f32), axis=0)
    push = col_ref[...] * drag_ref[0]
    chunks = LON // LANES
    for t in range(2):
        for k in range(chunks):
            columns = slice(k * LANES, (k + 1) * LANES)
            line = stress[t * chunks + k : t * chunks + k + 1, :]
            o_ref[t, 0, :, columns] = (d_ref[t, :, columns].astype(f32) + push * line).astype(bf16)


def local(
    spectral,
    legendre,
    wave_slot,
    coupling_in,
    interaction,
    bin_speed,
    momentum,
    wave_state,
    cell_index,
    edge_source,
    edge_target,
    surface_drag,
    mixing,
):
    slots, _, _, levels, degrees = spectral.shape
    lats = legendre.shape[1]
    all_slots = wave_slot.shape[0]
    owners = lax.axis_size("lat")
    columns = lax.axis_size("fld")
    bins, points = wave_state.shape
    fld = lax.axis_index("fld")
    shape = jax.ShapeDtypeStruct

    per = 4
    wave_row = wave_slot[None, :]
    sums, packed = pl.pallas_call(
        functools.partial(legendre_kernel, per, slots),
        grid=(slots // per,),
        in_specs=[
            SMEM,
            pl.BlockSpec((per, lats, degrees), lambda i: (i, 0, 0)),
            pl.BlockSpec((per, 2 * levels, degrees), lambda i: (i, 0, 0)),
        ],
        out_specs=[
            pl.BlockSpec((lats * slots, 2 * levels), lambda i: (0, 0)),
            pl.BlockSpec((owners // 2, 24, LANES), lambda i: (0, 0, 0)),
        ],
        out_shape=[shape((lats * slots, 2 * levels), bf16), shape((owners // 2, 24, LANES), bf16)],
        scratch_shapes=[
            pltpu.VMEM((lats * slots, LANES), f32),
            pltpu.VMEM((lats * slots, LANES), f32),
            pltpu.VMEM((LANES, LANES), f32),
        ],
        compiler_params=params(53),
        cost_estimate=cost(3e8, 5e6),
        name="legendre",
    )(wave_slot, legendre, spectral.reshape(slots, 2 * levels, degrees))
    same_core = [[2 * k + core for k in range(owners // 2)] for core in range(2)]
    own_part = lax.all_to_all(
        packed, "lat", split_axis=0, concat_axis=0, tiled=True, axis_index_groups=same_core
    )
    other_part = lax.ppermute(own_part, "lat", [(k, k ^ 1) for k in range(owners)])
    long = pl.pallas_call(
        long_kernel,
        in_specs=[VMEM],
        out_specs=VMEM,
        out_shape=shape((QUARTER, 2 * all_slots), bf16),
        compiler_params=params(10),
        cost_estimate=cost(6e6, 3e6),
        name="long",
    )(after(wave_row, own_part))

    tiles = owners * columns
    up = [(k, k + 1) for k in range(tiles - 1)]
    low = lax.ppermute(wave_state, ("lat", "fld"), up)
    high = lax.ppermute(wave_state, ("lat", "fld"), [(b, a) for a, b in up])

    lat_row = cell_index // LON
    rows = cell_index - lat_row * LON
    picked = pl.pallas_call(
        functools.partial(surface_kernel, all_slots),
        in_specs=[VMEM, VMEM, VMEM, VMEM, SMEM, VMEM],
        out_specs=VMEM,
        out_shape=shape((columns, points), f32),
        scratch_shapes=[pltpu.VMEM((LON, LANES), f32), pltpu.VMEM((columns * points, LANES), f32)],
        compiler_params=params(14),
        cost_estimate=cost(1e9, 4e6),
        name="surface",
    )(own_part, other_part, long, wave_row, rows, lat_row.reshape(columns, points))
    forcing = lax.all_to_all(picked, "fld", split_axis=0, concat_axis=0, tiled=True)

    own_cells = lax.dynamic_slice_in_dim(cell_index, fld * points, points)
    sign0 = 1 - 2 * ((own_cells >> 16) & 1)
    sign1 = 1 - 2 * (own_cells >> 17)
    codes = jnp.stack([((own_cells & 255) + 1) * sign0, (((own_cells >> 8) & 255) + 1) * sign1])
    codes = jnp.pad(codes.astype(f32).reshape(4, 64), ((0, 4), (64, 0)))
    main, tail, column = pl.pallas_call(
        functools.partial(mix_kernel, owners),
        in_specs=[SMEM, VMEM, VMEM],
        out_specs=[VMEM] * 3,
        out_shape=[
            shape((owners, 32, LANES), bf16),
            shape((owners, 8, LANES), f32),
            shape((levels, LANES), f32),
        ],
        scratch_shapes=[pltpu.VMEM((lats * slots, LANES), f32)] + [pltpu.VMEM((2 * levels, LANES), f32)] * 2,
        compiler_params=params(10),
        cost_estimate=cost(2e8, 2e6),
        name="mix",
    )(mixing, sums, codes)

    adv, base = pl.pallas_call(
        advect_kernel,
        in_specs=[VMEM] * 6 + [pl.BlockSpec(memory_space=pl.ANY)],
        out_specs=[VMEM] * 2,
        out_shape=[shape((bins, points), f32)] * 2,
        scratch_shapes=[pltpu.VMEM((bins, bins), bf16), pltpu.SemaphoreType.DMA],
        compiler_params=params(51),
        cost_estimate=cost(5e8, 4e6),
        name="advect",
    )(
        wave_state,
        low,
        high,
        after(edge_source[None, :], picked),
        edge_target[None, :],
        bin_speed[None, :],
        interaction,
    )

    wave_next, outgoing = pl.pallas_call(
        wave_kernel,
        in_specs=[VMEM] * 7,
        out_specs=[VMEM, VMEM],
        out_shape=[shape((bins, points), bf16), shape((owners, 40, LANES), bf16)],
        compiler_params=params(8),
        cost_estimate=cost(1e7, 2e6, bins * points),
        name="wave",
    )(forcing, coupling_in, adv, base, momentum[None, :], main, tail)
    bulk = lax.all_to_all(outgoing, "lat", split_axis=0, concat_axis=0, tiled=True)

    lat_rows = lats // owners
    partial = pl.pallas_call(
        scatter_kernel,
        in_specs=[VMEM],
        out_specs=VMEM,
        out_shape=shape((columns, lat_rows * LON // LANES, LANES), bf16),
        scratch_shapes=[pltpu.VMEM((owners * 8, LANES), f32)],
        compiler_params=params(8),
        cost_estimate=cost(1e8, 2e6),
        name="scatter",
    )(bulk)
    partials = lax.all_to_all(partial, "fld", split_axis=0, concat_axis=0, tiled=True)

    bulk = after(bulk, partial)
    wide = pl.pallas_call(
        wide_kernel,
        in_specs=[VMEM],
        out_specs=VMEM,
        out_shape=shape((2 * all_slots, QUARTER), bf16),
        compiler_params=params(10),
        cost_estimate=cost(6e6, 3e6),
        name="wide",
    )(after(wave_row, partial))
    mixed_rows = pl.pallas_call(
        functools.partial(synthesis_kernel, all_slots),
        in_specs=[VMEM, VMEM, VMEM],
        out_specs=VMEM,
        out_shape=shape((lat_rows, levels, LON), bf16),
        scratch_shapes=[pltpu.VMEM((owners * 32, LANES), f32), pltpu.VMEM((640, 2 * all_slots), bf16)],
        compiler_params=params(14),
        cost_estimate=cost(1.2e9, 6e6),
        name="synthesis",
    )(bulk, wave_row, wide)

    mixed = pl.pallas_call(
        final_kernel,
        in_specs=[VMEM, VMEM, VMEM, SMEM],
        out_specs=VMEM,
        out_shape=shape((lat_rows, 1, levels, LON), bf16),
        compiler_params=params(6),
        cost_estimate=cost(1e6, 3e6),
        name="final",
    )(mixed_rows, partials, column, surface_drag)
    return (mixed, wave_next)


def solution(mesh):
    in_specs = (
        P("lat", None, "fld", None, None),
        P("lat", None, None),
        P(),
        P(),
        P(),
        P(),
        P(),
        P(None, ("lat", "fld")),
        P("lat"),
        P(("lat", "fld")),
        P(("lat", "fld")),
        P("fld"),
        P(),
    )
    out_specs = (P("lat", "fld", None, None), P(None, ("lat", "fld")))
    return jax.shard_map(local, mesh=mesh, in_specs=in_specs, out_specs=out_specs, check_vma=False)
```

```python
import functools

import jax
import jax.numpy as jnp
from jax import lax
from jax.experimental import pallas as pl
from jax.experimental.pallas import tpu as pltpu
from jax.sharding import PartitionSpec as P

LON = 2560
RIM = 64
QUARTER = LON // 4
LANES = 128

time_step = 0.25

bf16 = jnp.bfloat16
f32 = jnp.float32
i32 = jnp.int32

NN = (((1,), (0,)), ((), ()))
NT = (((1,), (1,)), ((), ()))

VMEM = pl.BlockSpec(memory_space=pltpu.VMEM)
SMEM = pl.BlockSpec(memory_space=pltpu.SMEM)


def dot(a, b, dims=NN):
    return lax.dot_general(a, b, dims, preferred_element_type=f32)


def after(value, other):
    return lax.optimization_barrier((value, other))[0]


def lane_of(shape):
    return lax.broadcasted_iota(i32, shape, len(shape) - 1)


def params(mib, **more):
    return pltpu.CompilerParams(vmem_limit_bytes=mib << 20, **more)


def cost(flops, nbytes, trans=0):
    return pl.CostEstimate(flops=int(flops), bytes_accessed=int(nbytes), transcendentals=int(trans))


def legendre_kernel(per, slots, wave_ref, leg_ref, spec_ref, f_ref, x_ref, s0, s1, low):
    step = pl.program_id(0)
    lats, degrees = leg_ref.shape[1:]
    both = f_ref.shape[1]
    levels = both // 2

    @pl.when(step == 0)
    def _():
        low[...] = jnp.zeros_like(low)

    column = lane_of((1, degrees))
    lane = lane_of((lats, LANES))
    fill = jnp.zeros((lats, 2 * LANES - both), f32)
    first = lax.axis_index("lat") * slots
    picked = low[0:lats, :]
    for k in range(per):
        slot = step * per + k
        limit = degrees - lax.div(wave_ref[first + slot] * degrees, wave_ref.shape[0])
        weights = jnp.where(column < limit, leg_ref[k].astype(f32), 0.0).astype(bf16)
        sums = dot(weights, spec_ref[k], NT)
        s0[pl.ds(slot, lats, stride=slots), :] = sums[:, 0:LANES]
        s1[pl.ds(slot, lats, stride=slots), :] = jnp.concatenate([sums[:, LANES:], fill], axis=1)
        for c in range(2):
            lowest = jnp.broadcast_to(sums[:, (c + 1) * levels - 1 : (c + 1) * levels], (lats, LANES))
            picked = jnp.where(lane == c * slots + slot, lowest, picked)
    low[0:lats, :] = picked

    @pl.when(step == pl.num_programs(0) - 1)
    def _():
        f_ref[...] = jnp.concatenate([s0[...], s1[:, 0 : both - LANES]], axis=1).astype(bf16)
        turned = low[...].T
        tail = turned[24:32, :]
        lane8 = lane_of((8, LANES))
        rows = [
            jnp.where(lane8 < 96, turned[8 * h : 8 * h + 8, :], pltpu.roll(tail, 96 - 32 * h, 1))
            for h in range(3)
        ]
        packed = jnp.concatenate(rows, axis=0).astype(bf16)
        x_ref[...] = jnp.broadcast_to(packed[None], x_ref.shape)


def inverse(levels, mix_ref, col_ref, left, right):
    width = 2 * LANES
    lane = lax.broadcasted_iota(i32, (2, width), 1)
    start = lax.broadcasted_iota(i32, (2, width), 0) * levels
    unit = lane - start
    ratio, part = [], []
    for level in range(levels):
        below = jnp.full((2, width), mix_ref[level], f32)
        rhs = (unit == level).astype(f32)
        if level == 0:
            scale = 1.0 / (1.0 + below)
            part.append(rhs * scale)
        else:
            above = jnp.full((2, width), mix_ref[level - 1], f32)
            scale = 1.0 / (1.0 + below + above - above * ratio[-1])
            part.append((rhs + above * part[-1]) * scale)
        ratio.append(below * scale)
    solved = part[-1]
    for level in range(levels - 1, -1, -1):
        if level < levels - 1:
            solved = part[level] + ratio[level] * solved
        left[2 * level : 2 * level + 2, :] = solved[:, :LANES]
        right[2 * level : 2 * level + 2, :] = solved[:, LANES:]
    blocks = [
        jnp.concatenate([half[pl.ds(c, levels, stride=2), :] for half in (left, right)], axis=1) for c in range(2)
    ]
    col_ref[...] = jnp.broadcast_to(blocks[0][:, levels - 1 : levels], col_ref.shape)
    return jnp.concatenate(blocks, axis=0)


def mix_kernel(owners, mix_ref, f_ref, codes_ref, main_ref, tail_ref, col_ref, rest, left, right):
    mixer = inverse(f_ref.shape[1] // 2, mix_ref, col_ref, left, right)
    high = mixer.astype(bf16)
    sums = dot(f_ref[...], high) + dot(f_ref[...], (mixer - high.astype(f32)).astype(bf16))
    count = sums.shape[0]
    rest[...] = sums[:, LANES:]
    lane = lane_of((count // 4, LANES))
    tail = jnp.broadcast_to(codes_ref[...][None], (owners, 8, LANES)).reshape(count // 4, LANES)
    for g in range(4):
        piece = rest[pl.ds(g, count // 4, stride=4), :]
        if g:
            piece = pltpu.roll(piece, 16 * g, 1)
        tail = jnp.where((lane >= 16 * g) & (lane < 16 * g + 16), piece, tail)
    main_ref[...] = sums[:, :LANES].reshape(owners, count // owners, LANES).astype(bf16)
    tail_ref[...] = tail.reshape(owners, 8, LANES)


def waves(wave_ref):
    slots = wave_ref.shape[1]
    wave = wave_ref[...].astype(f32)

    def angles(count, unit):
        step = lax.broadcasted_iota(i32, (count, slots), 0).astype(f32) * float(unit)
        turn = step * wave
        turn = turn - float(LON) * jnp.floor(turn * (1.0 / LON) + 0.5)
        phase = turn * (2.0 * jnp.pi / LON)
        return jnp.cos(phase), jnp.sin(phase)

    ones = angles(16, 1)
    tens = angles(8, 16)
    parts = [added((tens[0][k : k + 1], tens[1][k : k + 1]), ones) for k in range(8)]
    return [jnp.concatenate([p[c] for p in parts], axis=0) for c in range(2)], angles(8, LANES)


def added(a, b):
    return a[0] * b[0] - a[1] * b[1], a[1] * b[0] + a[0] * b[1]


def long_kernel(wave_ref, long_ref):
    slots = wave_ref.shape[1]
    fine, coarse = waves(wave_ref)
    for a in range(QUARTER // LANES):
        c, s = added((coarse[0][a : a + 1], coarse[1][a : a + 1]), fine)
        rows = slice(a * LANES, (a + 1) * LANES)
        long_ref[rows, 0:slots] = c.astype(bf16)
        long_ref[rows, slots : 2 * slots] = (-s).astype(bf16)


def wide_kernel(wave_ref, wide_ref):
    slots = wave_ref.shape[1]
    fine, coarse = waves(wave_ref)
    for first in range(0, slots, LANES):
        mine = slice(first, first + LANES)
        turned = [x[:, mine].T for x in fine]
        for a in range(QUARTER // LANES):
            start = [jnp.broadcast_to(x[a : a + 1, mine], (LANES, LANES)).T for x in coarse]
            c, s = added(start, turned)
            columns = slice(a * LANES, (a + 1) * LANES)
            wide_ref[mine, columns] = c.astype(bf16)
            wide_ref[slots + first : slots + first + LANES, columns] = (-s).astype(bf16)


def quarters(wave):
    turns = wave & 3
    cos = jnp.where(turns == 0, 1.0, jnp.where(turns == 2, -1.0, 0.0))
    sin = jnp.where(turns == 1, 1.0, jnp.where(turns == 3, -1.0, 0.0))
    return cos, sin, jnp.where((turns & 1) == 0, 1.0, -1.0)


def turned(first, second, quarter):
    cos, sin, half = quarter
    fc, fs, sc, ss = first * cos, first * sin, second * cos, second * sin
    return [(first, second), (fc - ss, fs + sc), (first * half, second * half), (fc + ss, sc - fs)]


def unpacked(x_ref):
    peers = x_ref.shape[0]
    x = x_ref[...].astype(f32)
    lane = lane_of((peers, 8, LANES))
    tail = jnp.zeros((peers, 8, LANES), f32)
    for h in range(3):
        moved = pltpu.roll(x[:, 8 * h : 8 * h + 8, :].reshape(peers * 8, LANES), 32 + 32 * h, 1)
        tail = jnp.where((lane >= 32 * h) & (lane < 32 * h + 32), moved.reshape(peers, 8, LANES), tail)
    return x[:, 0:16, :], jnp.concatenate([x[:, 16:24, :], tail], axis=1)


def surface_kernel(slots, own_ref, other_ref, long_ref, wave_ref, row_ref, lat_ref, o_ref, surface, picked):
    first = lax.rem(lax.axis_index("lat"), 2) == 0
    own, other = unpacked(own_ref), unpacked(other_ref)
    real, imaginary = [
        jnp.stack([jnp.where(first, a, b), jnp.where(first, b, a)], axis=1).reshape(slots, LANES)
        for a, b in zip(own, other)
    ]
    pairs = turned(real, imaginary, [upright(x) for x in quarters(wave_ref[...])])
    coefficients = jnp.concatenate(
        [jnp.concatenate([p[c].astype(bf16) for p in pairs], axis=1) for c in range(2)], axis=0
    )
    values = dot(long_ref[...], coefficients).astype(bf16).astype(f32)
    for m in range(4):
        surface[m * QUARTER : (m + 1) * QUARTER, :] = values[:, m * LANES : (m + 1) * LANES]

    def fetch(block, carry):
        start = pl.multiple_of(block * LANES, LANES)
        window = picked.at[pl.ds(start, LANES), :]
        for u in range(LANES):
            window[u : u + 1, :] = surface[pl.ds(row_ref[start + u], 1), :]
        return carry

    lax.fori_loop(0, picked.shape[0] // LANES, fetch, 0)
    row = lax.broadcasted_iota(i32, (LANES, LANES), 0)
    diagonal = row == lane_of((LANES, LANES))
    for k in range(lat_ref.shape[0]):
        mine = slice(k * LANES, (k + 1) * LANES)
        hot = (row == lat_ref[k : k + 1, :]).astype(f32).astype(bf16)
        product = dot(picked[mine, :].astype(bf16), hot)
        o_ref[k : k + 1, :] = jnp.sum(jnp.where(diagonal, product, 0.0), axis=0, keepdims=True)


def upright(row_ref):
    row = row_ref[...]
    count = row.shape[1]
    parts = []
    for first in range(0, count, LANES):
        size = min(LANES, count - first)
        part = row[:, first : first + size]
        if size < LANES:
            part = jnp.concatenate([part, jnp.zeros((1, LANES - size), f32)], axis=1)
        parts.append(jnp.broadcast_to(part, (LANES, LANES)).T[0:size])
    return jnp.concatenate(parts, axis=0)


def advect_kernel(
    state_ref, low_ref, high_ref, source_ref, target_ref, speed_ref, inter_ref, adv_ref, base_ref, held, sem
):
    fetch = pltpu.make_async_copy(inter_ref, held, sem)
    fetch.start()
    edges = source_ref.shape[1]
    points = state_ref.shape[1]
    source_hot = (lax.broadcasted_iota(i32, (points + 2 * RIM, edges), 0) == source_ref[...]).astype(f32)
    target_hot = (lax.broadcasted_iota(i32, (points, edges), 0) == target_ref[...]).astype(f32)
    source_hot, target_hot = source_hot.astype(bf16), target_hot.astype(bf16)
    routes = dot(source_hot, target_hot, NT)
    counts = dot(jnp.ones((8, edges), bf16), target_hot, NT)[0:1, :]
    none = jnp.zeros((points - RIM, points), f32)
    tables = (
        (low_ref, jnp.concatenate([none, routes[0:RIM]], axis=0)),
        (state_ref, routes[RIM : RIM + points]),
        (high_ref, jnp.concatenate([routes[RIM + points :], none], axis=0)),
    )
    inflow = None
    for values, table in tables:
        high = table.astype(bf16)
        rest = (table - high.astype(f32)).astype(bf16)
        part = dot(values[...], high) + dot(values[...], rest)
        inflow = part if inflow is None else inflow + part
    current = state_ref[...].astype(f32)
    advected = current + upright(speed_ref) * (inflow - counts * current)
    squared = (advected * advected).astype(bf16)
    fetch.wait()
    transfer = dot(held[...], squared)
    adv_ref[...] = time_step * advected
    base_ref[...] = advected + time_step * transfer


def wave_kernel(forcing_ref, coupling_ref, adv_ref, base_ref, momentum_ref, main_ref, tail_ref, next_ref, o_ref):
    growth = jnp.tanh(dot(coupling_ref[...], forcing_ref[...].astype(bf16)))
    wave_new = base_ref[...] + growth * adv_ref[...]
    next_ref[...] = wave_new.astype(bf16)
    stress = jnp.sum(upright(momentum_ref) * growth * wave_new, axis=0, keepdims=True)
    stress = jnp.broadcast_to(stress, (8, LANES))
    high = stress.astype(bf16).astype(f32)
    low = stress - high
    row = lax.broadcasted_iota(i32, (8, LANES), 0)
    lane = lane_of((8, LANES))
    part = jnp.where(row < 6, high, low)
    part = jnp.where((row & 1) == 0, pltpu.roll(part, 64, 1), part)
    joined = jnp.where(((row >= 4) & (lane >= 64))[None], part[None], tail_ref[...])
    o_ref[...] = jnp.concatenate([main_ref[...].astype(f32), joined], axis=1).astype(bf16)


def synthesis_kernel(slots, y_ref, wave_ref, wide_ref, d_ref, rest, lhs):
    levels = d_ref.shape[1]
    peers = y_ref.shape[0]
    y = y_ref[...].astype(f32)
    main = y[:, 0:32, :]
    tail = y[:, 32:40, :].reshape(peers * 8, LANES)
    for g in range(4):
        rest[pl.ds(g, peers * 8, stride=4), :] = pltpu.roll(tail, LANES - 16 * g, 1) if g else tail
    quarter = quarters(wave_ref[...])
    others = rest[...].reshape(peers, 32, LANES)
    padded = 80
    fill = jnp.zeros((padded - levels, slots), f32)
    for t in range(2):
        a = main[:, 16 * t : 16 * t + 16, :].reshape(slots, LANES).T
        b = others[:, 16 * t : 16 * t + 16, :].reshape(slots, LANES).T
        first = a[0:levels]
        second = jnp.concatenate([a[levels:], b[0 : 2 * levels - LANES]], axis=0)
        for m, (p, q) in enumerate(turned(first, second, quarter)):
            rows = slice((t * 4 + m) * padded, (t * 4 + m + 1) * padded)
            lhs[rows, 0:slots] = jnp.concatenate([p, fill], axis=0).astype(bf16)
            lhs[rows, slots : 2 * slots] = jnp.concatenate([q, fill], axis=0).astype(bf16)
    for t in range(2):
        sums = dot(lhs[t * 4 * padded : (t + 1) * 4 * padded, :], wide_ref[...])
        for m in range(4):
            d_ref[t, :, m * QUARTER : (m + 1) * QUARTER] = sums[m * padded : m * padded + levels].astype(bf16)


def scatter_kernel(y_ref, o_ref, tails):
    peers = y_ref.shape[0]
    height = o_ref.shape[1]
    tails[...] = y_ref[...].astype(f32)[:, 32:40, :].reshape(peers * 8, LANES)
    lane = lane_of((peers, LANES))

    def line(k):
        left = pltpu.roll(tails[pl.ds(2 * k, peers, stride=8), :], 64, 1)
        return jnp.where(lane < 64, left, tails[pl.ds(2 * k + 1, peers, stride=8), :])

    v0, v1, high, low = [line(k) for k in range(4)]
    cell = (jnp.abs(v0) - 1.0) + 256.0 * (jnp.abs(v1) - 1.0)
    cell += jnp.where(v0 < 0, 65536.0, 0.0) + jnp.where(v1 < 0, 131072.0, 0.0)
    cell = cell.astype(i32) - lax.axis_index("lat") * (height * LANES)
    upper = cell >> 7
    at = cell & (LANES - 1)
    row = lax.broadcasted_iota(i32, (LANES, LANES), 0)
    sums = None
    for k in range(peers):
        one = slice(k, k + 1)
        inside = row[0:height] == upper[one]
        spread = jnp.concatenate([jnp.where(inside, high[one], 0.0), jnp.where(inside, low[one], 0.0)], axis=0)
        hot = (row == at[one]).astype(f32).astype(bf16)
        both = (spread.astype(bf16), hot)
        sums = [both] if sums is None else sums + [both]
    spread = jnp.concatenate([p[0] for p in sums], axis=1)
    hot = jnp.concatenate([p[1] for p in sums], axis=1)
    total = dot(spread, hot, NT)
    o_ref[...] = jnp.broadcast_to((total[0:height] + total[height:]).astype(bf16)[None], o_ref.shape)


def final_kernel(d_ref, part_ref, col_ref, drag_ref, o_ref):
    stress = jnp.sum(part_ref[...].astype(f32), axis=0)
    push = col_ref[...] * drag_ref[0]
    chunks = LON // LANES
    for t in range(2):
        for k in range(chunks):
            columns = slice(k * LANES, (k + 1) * LANES)
            line = stress[t * chunks + k : t * chunks + k + 1, :]
            o_ref[t, 0, :, columns] = (d_ref[t, :, columns].astype(f32) + push * line).astype(bf16)


def local(
    spectral,
    legendre,
    wave_slot,
    coupling_in,
    interaction,
    bin_speed,
    momentum,
    wave_state,
    cell_index,
    edge_source,
    edge_target,
    surface_drag,
    mixing,
):
    slots, _, _, levels, degrees = spectral.shape
    lats = legendre.shape[1]
    all_slots = wave_slot.shape[0]
    owners = lax.axis_size("lat")
    columns = lax.axis_size("fld")
    bins, points = wave_state.shape
    fld = lax.axis_index("fld")
    shape = jax.ShapeDtypeStruct

    per = slots // 2
    wave_row = wave_slot[None, :]
    sums, packed = pl.pallas_call(
        functools.partial(legendre_kernel, per, slots),
        grid_spec=pltpu.PrefetchScalarGridSpec(
            num_scalar_prefetch=1,
            grid=(slots // per,),
            in_specs=[
                pl.BlockSpec((per, lats, degrees), lambda i, _: (i, 0, 0)),
                pl.BlockSpec((per, 2 * levels, degrees), lambda i, _: (i, 0, 0)),
            ],
            out_specs=[
                pl.BlockSpec((lats * slots, 2 * levels), lambda i, _: (0, 0)),
                pl.BlockSpec((owners // 2, 24, LANES), lambda i, _: (0, 0, 0)),
            ],
            scratch_shapes=[
                pltpu.VMEM((lats * slots, LANES), f32),
                pltpu.VMEM((lats * slots, LANES), f32),
                pltpu.VMEM((LANES, LANES), f32),
            ],
        ),
        out_shape=[shape((lats * slots, 2 * levels), bf16), shape((owners // 2, 24, LANES), bf16)],
        compiler_params=params(54),
        cost_estimate=cost(3e8, 5e6),
        name="legendre",
    )(wave_slot, legendre, spectral.reshape(slots, 2 * levels, degrees))
    same_core = [[2 * k + core for k in range(owners // 2)] for core in range(2)]
    own_part = lax.all_to_all(
        packed, "lat", split_axis=0, concat_axis=0, tiled=True, axis_index_groups=same_core
    )
    other_part = lax.ppermute(own_part, "lat", [(k, k ^ 1) for k in range(owners)])
    long = pl.pallas_call(
        long_kernel,
        in_specs=[VMEM],
        out_specs=VMEM,
        out_shape=shape((QUARTER, 2 * all_slots), bf16),
        compiler_params=params(10),
        cost_estimate=cost(6e6, 3e6),
        name="long",
    )(after(wave_row, own_part))

    tiles = owners * columns
    up = [(k, k + 1) for k in range(tiles - 1)]
    low = lax.ppermute(wave_state, ("lat", "fld"), up)
    high = lax.ppermute(wave_state, ("lat", "fld"), [(b, a) for a, b in up])

    lat_row = cell_index // LON
    rows = cell_index - lat_row * LON
    picked = pl.pallas_call(
        functools.partial(surface_kernel, all_slots),
        in_specs=[VMEM, VMEM, VMEM, VMEM, SMEM, VMEM],
        out_specs=VMEM,
        out_shape=shape((columns, points), f32),
        scratch_shapes=[pltpu.VMEM((LON, LANES), f32), pltpu.VMEM((columns * points, LANES), f32)],
        compiler_params=params(14),
        cost_estimate=cost(1e9, 4e6),
        name="surface",
    )(own_part, other_part, long, wave_row, rows, lat_row.reshape(columns, points))
    forcing = lax.all_to_all(picked, "fld", split_axis=0, concat_axis=0, tiled=True)

    own_cells = lax.dynamic_slice_in_dim(cell_index, fld * points, points)
    sign0 = 1 - 2 * ((own_cells >> 16) & 1)
    sign1 = 1 - 2 * (own_cells >> 17)
    codes = jnp.stack([((own_cells & 255) + 1) * sign0, (((own_cells >> 8) & 255) + 1) * sign1])
    codes = jnp.pad(codes.astype(f32).reshape(4, 64), ((0, 4), (64, 0)))
    main, tail, column = pl.pallas_call(
        functools.partial(mix_kernel, owners),
        in_specs=[SMEM, VMEM, VMEM],
        out_specs=[VMEM] * 3,
        out_shape=[
            shape((owners, 32, LANES), bf16),
            shape((owners, 8, LANES), f32),
            shape((levels, LANES), f32),
        ],
        scratch_shapes=[pltpu.VMEM((lats * slots, LANES), f32)] + [pltpu.VMEM((2 * levels, LANES), f32)] * 2,
        compiler_params=params(10),
        cost_estimate=cost(2e8, 2e6),
        name="mix",
    )(mixing, after(sums, picked), codes)

    adv, base = pl.pallas_call(
        advect_kernel,
        in_specs=[VMEM] * 6 + [pl.BlockSpec(memory_space=pl.ANY)],
        out_specs=[VMEM] * 2,
        out_shape=[shape((bins, points), f32)] * 2,
        scratch_shapes=[pltpu.VMEM((bins, bins), bf16), pltpu.SemaphoreType.DMA],
        compiler_params=params(51),
        cost_estimate=cost(5e8, 4e6),
        name="advect",
    )(
        wave_state,
        low,
        high,
        after(edge_source[None, :], picked),
        edge_target[None, :],
        bin_speed[None, :],
        interaction,
    )

    wave_next, outgoing = pl.pallas_call(
        wave_kernel,
        in_specs=[VMEM] * 7,
        out_specs=[VMEM, VMEM],
        out_shape=[shape((bins, points), bf16), shape((owners, 40, LANES), bf16)],
        compiler_params=params(8),
        cost_estimate=cost(1e7, 2e6, bins * points),
        name="wave",
    )(forcing, coupling_in, adv, base, momentum[None, :], main, tail)
    bulk = lax.all_to_all(outgoing, "lat", split_axis=0, concat_axis=0, tiled=True)

    lat_rows = lats // owners
    partial = pl.pallas_call(
        scatter_kernel,
        in_specs=[VMEM],
        out_specs=VMEM,
        out_shape=shape((columns, lat_rows * LON // LANES, LANES), bf16),
        scratch_shapes=[pltpu.VMEM((owners * 8, LANES), f32)],
        compiler_params=params(8),
        cost_estimate=cost(1e8, 2e6),
        name="scatter",
    )(bulk)
    partials = lax.all_to_all(partial, "fld", split_axis=0, concat_axis=0, tiled=True)

    bulk = after(bulk, partial)
    wide = pl.pallas_call(
        wide_kernel,
        in_specs=[VMEM],
        out_specs=VMEM,
        out_shape=shape((2 * all_slots, QUARTER), bf16),
        compiler_params=params(10),
        cost_estimate=cost(6e6, 3e6),
        name="wide",
    )(after(wave_row, partial))
    mixed_rows = pl.pallas_call(
        functools.partial(synthesis_kernel, all_slots),
        in_specs=[VMEM, VMEM, VMEM],
        out_specs=VMEM,
        out_shape=shape((lat_rows, levels, LON), bf16),
        scratch_shapes=[pltpu.VMEM((owners * 32, LANES), f32), pltpu.VMEM((640, 2 * all_slots), bf16)],
        compiler_params=params(14),
        cost_estimate=cost(1.2e9, 6e6),
        name="synthesis",
    )(bulk, wave_row, wide)

    mixed = pl.pallas_call(
        final_kernel,
        in_specs=[VMEM, VMEM, VMEM, SMEM],
        out_specs=VMEM,
        out_shape=shape((lat_rows, 1, levels, LON), bf16),
        compiler_params=params(6),
        cost_estimate=cost(1e6, 3e6),
        name="final",
    )(mixed_rows, partials, column, surface_drag)
    return (mixed, wave_next)


def solution(mesh):
    in_specs = (
        P("lat", None, "fld", None, None),
        P("lat", None, None),
        P(),
        P(),
        P(),
        P(),
        P(),
        P(None, ("lat", "fld")),
        P("lat"),
        P(("lat", "fld")),
        P(("lat", "fld")),
        P("fld"),
        P(),
    )
    out_specs = (P("lat", "fld", None, None), P(None, ("lat", "fld")))
    return jax.shard_map(local, mesh=mesh, in_specs=in_specs, out_specs=out_specs, check_vma=False)
```

```python
import functools

import jax
import jax.numpy as jnp
from jax import lax
from jax.experimental import pallas as pl
from jax.experimental.pallas import tpu as pltpu
from jax.sharding import PartitionSpec as P

LON = 2560
RIM = 64
QUARTER = LON // 4
LANES = 128

time_step = 0.25

bf16 = jnp.bfloat16
f32 = jnp.float32
i32 = jnp.int32

NN = (((1,), (0,)), ((), ()))
NT = (((1,), (1,)), ((), ()))

VMEM = pl.BlockSpec(memory_space=pltpu.VMEM)
SMEM = pl.BlockSpec(memory_space=pltpu.SMEM)


def dot(a, b, dims=NN):
    return lax.dot_general(a, b, dims, preferred_element_type=f32)


def after(value, other):
    return lax.optimization_barrier((value, other))[0]


def lane_of(shape):
    return lax.broadcasted_iota(i32, shape, len(shape) - 1)


def params(mib, **more):
    return pltpu.CompilerParams(vmem_limit_bytes=mib << 20, **more)


def cost(flops, nbytes, trans=0):
    return pl.CostEstimate(flops=int(flops), bytes_accessed=int(nbytes), transcendentals=int(trans))


def legendre_kernel(per, slots, wave_ref, leg_ref, spec_ref, f_ref, x_ref, s0, s1, low):
    step = pl.program_id(0)
    lats, degrees = leg_ref.shape[1:]
    both = f_ref.shape[1]
    levels = both // 2

    @pl.when(step == 0)
    def _():
        low[...] = jnp.zeros_like(low)

    column = lane_of((1, degrees))
    lane = lane_of((lats, LANES))
    fill = jnp.zeros((lats, 2 * LANES - both), f32)
    first = lax.axis_index("lat") * slots
    picked = low[0:lats, :]
    for k in range(per):
        slot = step * per + k
        limit = degrees - lax.div(wave_ref[first + slot] * degrees, wave_ref.shape[0])
        weights = jnp.where(column < limit, leg_ref[k].astype(f32), 0.0).astype(bf16)
        sums = dot(weights, spec_ref[k], NT)
        s0[pl.ds(slot, lats, stride=slots), :] = sums[:, 0:LANES]
        s1[pl.ds(slot, lats, stride=slots), :] = jnp.concatenate([sums[:, LANES:], fill], axis=1)
        for c in range(2):
            lowest = jnp.broadcast_to(sums[:, (c + 1) * levels - 1 : (c + 1) * levels], (lats, LANES))
            picked = jnp.where(lane == c * slots + slot, lowest, picked)
    low[0:lats, :] = picked

    @pl.when(step == pl.num_programs(0) - 1)
    def _():
        f_ref[...] = jnp.concatenate([s0[...], s1[:, 0 : both - LANES]], axis=1).astype(bf16)
        turned = low[...].T
        tail = turned[24:32, :]
        lane8 = lane_of((8, LANES))
        rows = [
            jnp.where(lane8 < 96, turned[8 * h : 8 * h + 8, :], pltpu.roll(tail, 96 - 32 * h, 1))
            for h in range(3)
        ]
        packed = jnp.concatenate(rows, axis=0).astype(bf16)
        x_ref[...] = jnp.broadcast_to(packed[None], x_ref.shape)


def inverse(levels, mix_ref, col_ref, left, right):
    width = 2 * LANES
    lane = lax.broadcasted_iota(i32, (2, width), 1)
    start = lax.broadcasted_iota(i32, (2, width), 0) * levels
    unit = lane - start
    ratio, part = [], []
    for level in range(levels):
        below = jnp.full((2, width), mix_ref[level], f32)
        rhs = (unit == level).astype(f32)
        if level == 0:
            scale = 1.0 / (1.0 + below)
            part.append(rhs * scale)
        else:
            above = jnp.full((2, width), mix_ref[level - 1], f32)
            scale = 1.0 / (1.0 + below + above - above * ratio[-1])
            part.append((rhs + above * part[-1]) * scale)
        ratio.append(below * scale)
    solved = part[-1]
    for level in range(levels - 1, -1, -1):
        if level < levels - 1:
            solved = part[level] + ratio[level] * solved
        left[2 * level : 2 * level + 2, :] = solved[:, :LANES]
        right[2 * level : 2 * level + 2, :] = solved[:, LANES:]
    blocks = [
        jnp.concatenate([half[pl.ds(c, levels, stride=2), :] for half in (left, right)], axis=1) for c in range(2)
    ]
    col_ref[...] = jnp.broadcast_to(blocks[0][:, levels - 1 : levels], col_ref.shape)
    return jnp.concatenate(blocks, axis=0)


def mix_kernel(owners, mix_ref, f_ref, codes_ref, main_ref, tail_ref, col_ref, rest, left, right):
    mixer = inverse(f_ref.shape[1] // 2, mix_ref, col_ref, left, right)
    high = mixer.astype(bf16)
    sums = dot(f_ref[...], high) + dot(f_ref[...], (mixer - high.astype(f32)).astype(bf16))
    count = sums.shape[0]
    rest[...] = sums[:, LANES:]
    lane = lane_of((count // 4, LANES))
    tail = jnp.broadcast_to(codes_ref[...][None], (owners, 8, LANES)).reshape(count // 4, LANES)
    for g in range(4):
        piece = rest[pl.ds(g, count // 4, stride=4), :]
        if g:
            piece = pltpu.roll(piece, 16 * g, 1)
        tail = jnp.where((lane >= 16 * g) & (lane < 16 * g + 16), piece, tail)
    main_ref[...] = sums[:, :LANES].reshape(owners, count // owners, LANES).astype(bf16)
    tail_ref[...] = tail.reshape(owners, 8, LANES)


def waves(wave_ref):
    slots = wave_ref.shape[1]
    wave = wave_ref[...].astype(f32)

    def angles(count, unit):
        step = lax.broadcasted_iota(i32, (count, slots), 0).astype(f32) * float(unit)
        turn = step * wave
        turn = turn - float(LON) * jnp.floor(turn * (1.0 / LON) + 0.5)
        phase = turn * (2.0 * jnp.pi / LON)
        return jnp.cos(phase), jnp.sin(phase)

    ones = angles(16, 1)
    tens = angles(8, 16)
    parts = [added((tens[0][k : k + 1], tens[1][k : k + 1]), ones) for k in range(8)]
    return [jnp.concatenate([p[c] for p in parts], axis=0) for c in range(2)], angles(8, LANES)


def added(a, b):
    return a[0] * b[0] - a[1] * b[1], a[1] * b[0] + a[0] * b[1]


def long_kernel(wave_ref, long_ref):
    slots = wave_ref.shape[1]
    fine, coarse = waves(wave_ref)
    for a in range(QUARTER // LANES):
        c, s = added((coarse[0][a : a + 1], coarse[1][a : a + 1]), fine)
        rows = slice(a * LANES, (a + 1) * LANES)
        long_ref[rows, 0:slots] = c.astype(bf16)
        long_ref[rows, slots : 2 * slots] = (-s).astype(bf16)


def wide_kernel(wave_ref, wide_ref):
    slots = wave_ref.shape[1]
    fine, coarse = waves(wave_ref)
    for first in range(0, slots, LANES):
        mine = slice(first, first + LANES)
        turned = [x[:, mine].T for x in fine]
        for a in range(QUARTER // LANES):
            start = [jnp.broadcast_to(x[a : a + 1, mine], (LANES, LANES)).T for x in coarse]
            c, s = added(start, turned)
            columns = slice(a * LANES, (a + 1) * LANES)
            wide_ref[mine, columns] = c.astype(bf16)
            wide_ref[slots + first : slots + first + LANES, columns] = (-s).astype(bf16)


def quarters(wave):
    turns = wave & 3
    cos = jnp.where(turns == 0, 1.0, jnp.where(turns == 2, -1.0, 0.0))
    sin = jnp.where(turns == 1, 1.0, jnp.where(turns == 3, -1.0, 0.0))
    return cos, sin, jnp.where((turns & 1) == 0, 1.0, -1.0)


def turned(first, second, quarter):
    cos, sin, half = quarter
    fc, fs, sc, ss = first * cos, first * sin, second * cos, second * sin
    return [(first, second), (fc - ss, fs + sc), (first * half, second * half), (fc + ss, sc - fs)]


def unpacked(x_ref):
    peers = x_ref.shape[0]
    x = x_ref[...].astype(f32)
    lane = lane_of((peers, 8, LANES))
    tail = jnp.zeros((peers, 8, LANES), f32)
    for h in range(3):
        moved = pltpu.roll(x[:, 8 * h : 8 * h + 8, :].reshape(peers * 8, LANES), 32 + 32 * h, 1)
        tail = jnp.where((lane >= 32 * h) & (lane < 32 * h + 32), moved.reshape(peers, 8, LANES), tail)
    return x[:, 0:16, :], jnp.concatenate([x[:, 16:24, :], tail], axis=1)


def surface_kernel(slots, own_ref, other_ref, long_ref, wave_ref, row_ref, lat_ref, o_ref, surface, picked):
    real, imaginary = [
        jnp.concatenate([a, b], axis=0).reshape(slots, LANES) for a, b in zip(unpacked(own_ref), unpacked(other_ref))
    ]
    pairs = turned(real, imaginary, [upright(x) for x in quarters(wave_ref[...])])
    coefficients = jnp.concatenate(
        [jnp.concatenate([p[c].astype(bf16) for p in pairs], axis=1) for c in range(2)], axis=0
    )
    values = dot(long_ref[...], coefficients).astype(bf16).astype(f32)
    for m in range(4):
        surface[m * QUARTER : (m + 1) * QUARTER, :] = values[:, m * LANES : (m + 1) * LANES]

    def fetch(block, carry):
        start = pl.multiple_of(block * LANES, LANES)
        window = picked.at[pl.ds(start, LANES), :]
        for u in range(LANES):
            window[u : u + 1, :] = surface[pl.ds(row_ref[start + u], 1), :]
        return carry

    lax.fori_loop(0, picked.shape[0] // LANES, fetch, 0)
    row = lax.broadcasted_iota(i32, (LANES, LANES), 0)
    diagonal = row == lane_of((LANES, LANES))
    for k in range(lat_ref.shape[0]):
        mine = slice(k * LANES, (k + 1) * LANES)
        hot = (row == lat_ref[k : k + 1, :]).astype(f32).astype(bf16)
        product = dot(picked[mine, :].astype(bf16), hot)
        o_ref[k : k + 1, :] = jnp.sum(jnp.where(diagonal, product, 0.0), axis=0, keepdims=True)


def upright(row_ref):
    row = row_ref[...]
    count = row.shape[1]
    parts = []
    for first in range(0, count, LANES):
        size = min(LANES, count - first)
        part = row[:, first : first + size]
        if size < LANES:
            part = jnp.concatenate([part, jnp.zeros((1, LANES - size), f32)], axis=1)
        parts.append(jnp.broadcast_to(part, (LANES, LANES)).T[0:size])
    return jnp.concatenate(parts, axis=0)


def advect_kernel(
    state_ref, low_ref, high_ref, source_ref, target_ref, speed_ref, inter_ref, adv_ref, base_ref, held, sem
):
    fetch = pltpu.make_async_copy(inter_ref, held, sem)
    fetch.start()
    edges = source_ref.shape[1]
    points = state_ref.shape[1]
    source_hot = (lax.broadcasted_iota(i32, (points + 2 * RIM, edges), 0) == source_ref[...]).astype(f32)
    target_hot = (lax.broadcasted_iota(i32, (points, edges), 0) == target_ref[...]).astype(f32)
    source_hot, target_hot = source_hot.astype(bf16), target_hot.astype(bf16)
    routes = dot(source_hot, target_hot, NT)
    counts = dot(jnp.ones((8, edges), bf16), target_hot, NT)[0:1, :]
    none = jnp.zeros((points - RIM, points), f32)
    tables = (
        (low_ref, jnp.concatenate([none, routes[0:RIM]], axis=0)),
        (state_ref, routes[RIM : RIM + points]),
        (high_ref, jnp.concatenate([routes[RIM + points :], none], axis=0)),
    )
    inflow = None
    for values, table in tables:
        high = table.astype(bf16)
        rest = (table - high.astype(f32)).astype(bf16)
        part = dot(values[...], high) + dot(values[...], rest)
        inflow = part if inflow is None else inflow + part
    current = state_ref[...].astype(f32)
    advected = current + upright(speed_ref) * (inflow - counts * current)
    squared = (advected * advected).astype(bf16)
    fetch.wait()
    transfer = dot(held[...], squared)
    adv_ref[...] = time_step * advected
    base_ref[...] = advected + time_step * transfer


def wave_kernel(forcing_ref, coupling_ref, adv_ref, base_ref, momentum_ref, main_ref, tail_ref, next_ref, o_ref):
    growth = jnp.tanh(dot(coupling_ref[...], forcing_ref[...].astype(bf16)))
    wave_new = base_ref[...] + growth * adv_ref[...]
    next_ref[...] = wave_new.astype(bf16)
    stress = jnp.sum(upright(momentum_ref) * growth * wave_new, axis=0, keepdims=True)
    stress = jnp.broadcast_to(stress, (8, LANES))
    high = stress.astype(bf16).astype(f32)
    low = stress - high
    row = lax.broadcasted_iota(i32, (8, LANES), 0)
    lane = lane_of((8, LANES))
    part = jnp.where(row < 6, high, low)
    part = jnp.where((row & 1) == 0, pltpu.roll(part, 64, 1), part)
    joined = jnp.where(((row >= 4) & (lane >= 64))[None], part[None], tail_ref[...])
    o_ref[...] = jnp.concatenate([main_ref[...].astype(f32), joined], axis=1).astype(bf16)


def synthesis_kernel(slots, y_ref, wave_ref, wide_ref, d_ref, rest, lhs):
    levels = d_ref.shape[1]
    peers = y_ref.shape[0]
    y = y_ref[...].astype(f32)
    main = y[:, 0:32, :]
    tail = y[:, 32:40, :].reshape(peers * 8, LANES)
    for g in range(4):
        rest[pl.ds(g, peers * 8, stride=4), :] = pltpu.roll(tail, LANES - 16 * g, 1) if g else tail
    quarter = quarters(wave_ref[...])
    others = rest[...].reshape(peers, 32, LANES)
    padded = 80
    fill = jnp.zeros((padded - levels, slots), f32)
    for t in range(2):
        a = main[:, 16 * t : 16 * t + 16, :].reshape(slots, LANES).T
        b = others[:, 16 * t : 16 * t + 16, :].reshape(slots, LANES).T
        first = a[0:levels]
        second = jnp.concatenate([a[levels:], b[0 : 2 * levels - LANES]], axis=0)
        for m, (p, q) in enumerate(turned(first, second, quarter)):
            rows = slice((t * 4 + m) * padded, (t * 4 + m + 1) * padded)
            lhs[rows, 0:slots] = jnp.concatenate([p, fill], axis=0).astype(bf16)
            lhs[rows, slots : 2 * slots] = jnp.concatenate([q, fill], axis=0).astype(bf16)
    for t in range(2):
        sums = dot(lhs[t * 4 * padded : (t + 1) * 4 * padded, :], wide_ref[...])
        for m in range(4):
            d_ref[t, :, m * QUARTER : (m + 1) * QUARTER] = sums[m * padded : m * padded + levels].astype(bf16)


def scatter_kernel(y_ref, o_ref, tails):
    peers = y_ref.shape[0]
    height = o_ref.shape[1]
    tails[...] = y_ref[...].astype(f32)[:, 32:40, :].reshape(peers * 8, LANES)
    lane = lane_of((peers, LANES))

    def line(k):
        left = pltpu.roll(tails[pl.ds(2 * k, peers, stride=8), :], 64, 1)
        return jnp.where(lane < 64, left, tails[pl.ds(2 * k + 1, peers, stride=8), :])

    v0, v1, high, low = [line(k) for k in range(4)]
    cell = (jnp.abs(v0) - 1.0) + 256.0 * (jnp.abs(v1) - 1.0)
    cell += jnp.where(v0 < 0, 65536.0, 0.0) + jnp.where(v1 < 0, 131072.0, 0.0)
    cell = cell.astype(i32) - lax.axis_index("lat") * (height * LANES)
    upper = cell >> 7
    at = cell & (LANES - 1)
    row = lax.broadcasted_iota(i32, (LANES, LANES), 0)
    sums = None
    for k in range(peers):
        one = slice(k, k + 1)
        inside = row[0:height] == upper[one]
        spread = jnp.concatenate([jnp.where(inside, high[one], 0.0), jnp.where(inside, low[one], 0.0)], axis=0)
        hot = (row == at[one]).astype(f32).astype(bf16)
        both = (spread.astype(bf16), hot)
        sums = [both] if sums is None else sums + [both]
    spread = jnp.concatenate([p[0] for p in sums], axis=1)
    hot = jnp.concatenate([p[1] for p in sums], axis=1)
    total = dot(spread, hot, NT)
    o_ref[...] = jnp.broadcast_to((total[0:height] + total[height:]).astype(bf16)[None], o_ref.shape)


def final_kernel(d_ref, part_ref, col_ref, drag_ref, o_ref):
    stress = jnp.sum(part_ref[...].astype(f32), axis=0)
    push = col_ref[...] * drag_ref[0]
    chunks = LON // LANES
    for t in range(2):
        for k in range(chunks):
            columns = slice(k * LANES, (k + 1) * LANES)
            line = stress[t * chunks + k : t * chunks + k + 1, :]
            o_ref[t, 0, :, columns] = (d_ref[t, :, columns].astype(f32) + push * line).astype(bf16)


def local(
    spectral,
    legendre,
    wave_slot,
    coupling_in,
    interaction,
    bin_speed,
    momentum,
    wave_state,
    cell_index,
    edge_source,
    edge_target,
    surface_drag,
    mixing,
):
    slots, _, _, levels, degrees = spectral.shape
    lats = legendre.shape[1]
    all_slots = wave_slot.shape[0]
    owners = lax.axis_size("lat")
    columns = lax.axis_size("fld")
    bins, points = wave_state.shape
    fld = lax.axis_index("fld")
    shape = jax.ShapeDtypeStruct

    per = slots // 2
    wave_row = wave_slot[None, :]
    sums, packed = pl.pallas_call(
        functools.partial(legendre_kernel, per, slots),
        grid_spec=pltpu.PrefetchScalarGridSpec(
            num_scalar_prefetch=1,
            grid=(slots // per,),
            in_specs=[
                pl.BlockSpec((per, lats, degrees), lambda i, _: (i, 0, 0)),
                pl.BlockSpec((per, 2 * levels, degrees), lambda i, _: (i, 0, 0)),
            ],
            out_specs=[
                pl.BlockSpec((lats * slots, 2 * levels), lambda i, _: (0, 0)),
                pl.BlockSpec((owners // 2, 24, LANES), lambda i, _: (0, 0, 0)),
            ],
            scratch_shapes=[
                pltpu.VMEM((lats * slots, LANES), f32),
                pltpu.VMEM((lats * slots, LANES), f32),
                pltpu.VMEM((LANES, LANES), f32),
            ],
        ),
        out_shape=[shape((lats * slots, 2 * levels), bf16), shape((owners // 2, 24, LANES), bf16)],
        compiler_params=params(54),
        cost_estimate=cost(3e8, 5e6),
        name="legendre",
    )(wave_slot, legendre, spectral.reshape(slots, 2 * levels, degrees))
    same_core = [[2 * k + core for k in range(owners // 2)] for core in range(2)]
    own_part = lax.all_to_all(
        packed, "lat", split_axis=0, concat_axis=0, tiled=True, axis_index_groups=same_core
    )
    other_part = lax.ppermute(own_part, "lat", [(k, k ^ 1) for k in range(owners)])
    by_core = wave_slot.reshape(owners // 2, 2, slots).transpose(1, 0, 2).reshape(2, all_slots // 2)
    by_core = jnp.where(lax.axis_index("lat") % 2 == 0, by_core, by_core[::-1]).reshape(1, all_slots)
    long = pl.pallas_call(
        long_kernel,
        in_specs=[VMEM],
        out_specs=VMEM,
        out_shape=shape((QUARTER, 2 * all_slots), bf16),
        compiler_params=params(10),
        cost_estimate=cost(6e6, 3e6),
        name="long",
    )(after(by_core, own_part))

    tiles = owners * columns
    up = [(k, k + 1) for k in range(tiles - 1)]
    low = lax.ppermute(wave_state, ("lat", "fld"), up)
    high = lax.ppermute(wave_state, ("lat", "fld"), [(b, a) for a, b in up])

    lat_row = cell_index // LON
    rows = cell_index - lat_row * LON
    picked = pl.pallas_call(
        functools.partial(surface_kernel, all_slots),
        in_specs=[VMEM, VMEM, VMEM, VMEM, SMEM, VMEM],
        out_specs=VMEM,
        out_shape=shape((columns, points), f32),
        scratch_shapes=[pltpu.VMEM((LON, LANES), f32), pltpu.VMEM((columns * points, LANES), f32)],
        compiler_params=params(14),
        cost_estimate=cost(1e9, 4e6),
        name="surface",
    )(own_part, other_part, long, by_core, rows, lat_row.reshape(columns, points))
    forcing = lax.all_to_all(picked, "fld", split_axis=0, concat_axis=0, tiled=True)

    own_cells = lax.dynamic_slice_in_dim(cell_index, fld * points, points)
    sign0 = 1 - 2 * ((own_cells >> 16) & 1)
    sign1 = 1 - 2 * (own_cells >> 17)
    codes = jnp.stack([((own_cells & 255) + 1) * sign0, (((own_cells >> 8) & 255) + 1) * sign1])
    codes = jnp.pad(codes.astype(f32).reshape(4, 64), ((0, 4), (64, 0)))
    main, tail, column = pl.pallas_call(
        functools.partial(mix_kernel, owners),
        in_specs=[SMEM, VMEM, VMEM],
        out_specs=[VMEM] * 3,
        out_shape=[
            shape((owners, 32, LANES), bf16),
            shape((owners, 8, LANES), f32),
            shape((levels, LANES), f32),
        ],
        scratch_shapes=[pltpu.VMEM((lats * slots, LANES), f32)] + [pltpu.VMEM((2 * levels, LANES), f32)] * 2,
        compiler_params=params(10),
        cost_estimate=cost(2e8, 2e6),
        name="mix",
    )(mixing, after(sums, picked), codes)

    adv, base = pl.pallas_call(
        advect_kernel,
        in_specs=[VMEM] * 6 + [pl.BlockSpec(memory_space=pl.ANY)],
        out_specs=[VMEM] * 2,
        out_shape=[shape((bins, points), f32)] * 2,
        scratch_shapes=[pltpu.VMEM((bins, bins), bf16), pltpu.SemaphoreType.DMA],
        compiler_params=params(51),
        cost_estimate=cost(5e8, 4e6),
        name="advect",
    )(
        wave_state,
        low,
        high,
        after(edge_source[None, :], picked),
        edge_target[None, :],
        bin_speed[None, :],
        interaction,
    )

    wave_next, outgoing = pl.pallas_call(
        wave_kernel,
        in_specs=[VMEM] * 7,
        out_specs=[VMEM, VMEM],
        out_shape=[shape((bins, points), bf16), shape((owners, 40, LANES), bf16)],
        compiler_params=params(8),
        cost_estimate=cost(1e7, 2e6, bins * points),
        name="wave",
    )(forcing, coupling_in, adv, base, momentum[None, :], main, tail)
    bulk = lax.all_to_all(outgoing, "lat", split_axis=0, concat_axis=0, tiled=True)

    lat_rows = lats // owners
    partial = pl.pallas_call(
        scatter_kernel,
        in_specs=[VMEM],
        out_specs=VMEM,
        out_shape=shape((columns, lat_rows * LON // LANES, LANES), bf16),
        scratch_shapes=[pltpu.VMEM((owners * 8, LANES), f32)],
        compiler_params=params(8),
        cost_estimate=cost(1e8, 2e6),
        name="scatter",
    )(bulk)
    partials = lax.all_to_all(partial, "fld", split_axis=0, concat_axis=0, tiled=True)

    bulk = after(bulk, partial)
    wide = pl.pallas_call(
        wide_kernel,
        in_specs=[VMEM],
        out_specs=VMEM,
        out_shape=shape((2 * all_slots, QUARTER), bf16),
        compiler_params=params(10),
        cost_estimate=cost(6e6, 3e6),
        name="wide",
    )(after(wave_row, partial))
    mixed_rows = pl.pallas_call(
        functools.partial(synthesis_kernel, all_slots),
        in_specs=[VMEM, VMEM, VMEM],
        out_specs=VMEM,
        out_shape=shape((lat_rows, levels, LON), bf16),
        scratch_shapes=[pltpu.VMEM((owners * 32, LANES), f32), pltpu.VMEM((640, 2 * all_slots), bf16)],
        compiler_params=params(14),
        cost_estimate=cost(1.2e9, 6e6),
        name="synthesis",
    )(bulk, wave_row, wide)

    mixed = pl.pallas_call(
        final_kernel,
        in_specs=[VMEM, VMEM, VMEM, SMEM],
        out_specs=VMEM,
        out_shape=shape((lat_rows, 1, levels, LON), bf16),
        compiler_params=params(6),
        cost_estimate=cost(1e6, 3e6),
        name="final",
    )(mixed_rows, partials, column, surface_drag)
    return (mixed, wave_next)


def solution(mesh):
    in_specs = (
        P("lat", None, "fld", None, None),
        P("lat", None, None),
        P(),
        P(),
        P(),
        P(),
        P(),
        P(None, ("lat", "fld")),
        P("lat"),
        P(("lat", "fld")),
        P(("lat", "fld")),
        P("fld"),
        P(),
    )
    out_specs = (P("lat", "fld", None, None), P(None, ("lat", "fld")))
    return jax.shard_map(local, mesh=mesh, in_specs=in_specs, out_specs=out_specs, check_vma=False)
```
